32 devices in a mesh: feat: 16 (over z, y, core), width: 2 (over x).
Axes of the slice: x: 2, y: 2, z: 4, core: 2. Of those that a mesh axis runs over, the one named last changes fastest.
Arguments:
- residual: bfloat16 [2, 448, 3584], P(None, None, 'width'), may hold values from -6 to 6
- targets: bfloat16 [2, 448, 3584], P(None, None, 'width'), may hold values from -6 to 6
- encoder: bfloat16 [3584, 32768], P('width', 'feat'), may hold values from -0.09375 to 0.09375
- biases: bfloat16 [32768], P('feat'), may hold values from -3 to 3
- same_decoder: bfloat16 [32768, 3584], P('feat', 'width'), may hold values from -0.03125 to 0.03125
- next_decoder: bfloat16 [16384, 3584], P('feat', 'width'), may hold values from -0.03125 to 0.03125
- encoder_first: bfloat16 [3584, 32768], P('width', 'feat'), may hold values from -24 to 24
- encoder_second: bfloat16 [3584, 32768], P('width', 'feat'), may hold values from 4 to 64
- biases_first: bfloat16 [32768], P('feat'), may hold values from -24 to 24
- biases_second: bfloat16 [32768], P('feat'), may hold values from 4 to 64
- same_first: bfloat16 [32768, 3584], P('feat', 'width'), may hold values from -24 to 24
- same_second: bfloat16 [32768, 3584], P('feat', 'width'), may hold values from 4 to 64
- next_first: bfloat16 [16384, 3584], P('feat', 'width'), may hold values from -24 to 24
- next_second: bfloat16 [16384, 3584], P('feat', 'width'), may hold values from 4 to 64
Outputs:
- updated_encoder: bfloat16 [3584, 32768], P('width', 'feat')
- updated_biases: bfloat16 [32768], P('feat')
- updated_same: bfloat16 [32768, 3584], P('feat', 'width')
- updated_next: bfloat16 [16384, 3584], P('feat', 'width')
- encoder_moment: bfloat16 [3584, 32768], P('width', 'feat')
- encoder_square: bfloat16 [3584, 32768], P('width', 'feat')
- biases_moment: bfloat16 [32768], P('feat')
- biases_square: bfloat16 [32768], P('feat')
- same_moment: bfloat16 [32768, 3584], P('feat', 'width')
- same_square: bfloat16 [32768, 3584], P('feat', 'width')
- next_moment: bfloat16 [16384, 3584], P('feat', 'width')
- next_square: bfloat16 [16384, 3584], P('feat', 'width')
The draws below stay inside these ranges and needn't reach their ends.
All inputs are finite; a program needn't handle non-finite values.
Results may differ from the reference program's by a relative error of at most 0.0055.
Values may be sent and summed in bfloat16 or wider, within the bound.
No kernel may reach another device: no remote copies, remote signals or barrier semaphores. Data moves between devices by JAX's collectives and lax.ppermute only.
A program may use at most 256 MiB of HBM per device.

```python
import math
import jax
import jax.numpy as jnp
from jax import lax

D = 3584
F = 16384
L = 2
TOK = 448
STEPS = 100
FD = 2048


def block_levels(stream_key, shape, shards, least, largest):
    def one(position, blocks):
        draws = jax.random.uniform(jax.random.fold_in(jax.random.fold_in(stream_key, 6), position), (blocks,), jnp.float32, least / len(shards), largest / len(shards))
        return jnp.repeat(jnp.exp(draws), shape[position] // blocks).reshape((-1,) + (1,) * (len(shape) - position - 1))

    gain = one(*shards[0])
    for cut in shards[1:]:
        gain = gain * one(*cut)
    return gain


def centred(key, shape, spread, limit, split=(), kind=jnp.bfloat16):
    entries = jax.random.normal(key, shape, jnp.float32) * spread
    if len(split) > 0:
        entries = block_levels(key, shape, split, -0.22, 0.18) * entries
    return jnp.clip(entries, min=-limit, max=limit).astype(kind)


def setup_inputs(seed: int = 0) -> dict:
    arg_keys = jax.random.split(jax.random.key(seed), 15)
    residual = centred(arg_keys[0], (L, TOK, D), 1.0, 6.0, ((2, 2),))
    targets = centred(arg_keys[1], (L, TOK, D), 1.0, 6.0, ((2, 2),))
    encoder = centred(arg_keys[2], (D, L * F), D ** -0.5, 0.09375, ((0, 2), (1, 16)))
    biases = centred(arg_keys[3], (L * F,), 0.5, 3.0, ((0, 16),))
    same_decoder = centred(arg_keys[4], (L * F, D), (2 * F) ** -0.5, 0.03125, ((0, 16), (1, 2)))
    next_decoder = centred(arg_keys[5], (F, D), (2 * F) ** -0.5, 0.03125, ((0, 16), (1, 2)))
    encoder_first = centred(arg_keys[6], (D, L * F), 4.0, 24.0, ((0, 2), (1, 16)))
    encoder_second = jnp.clip(jnp.exp(math.log(64.0) - 2.7725887 * jax.random.uniform(arg_keys[7], (D, L * F), jnp.float32) ** block_levels(arg_keys[7], (D, L * F), ((0, 2), (1, 16)), -0.2, 0.2)), 4.0, 64.0).astype(jnp.bfloat16)
    biases_first = centred(arg_keys[8], (L * F,), 4.0, 24.0, ((0, 16),))
    biases_second = jnp.clip(jnp.exp(math.log(64.0) - 2.7725887 * jax.random.uniform(arg_keys[9], (L * F,), jnp.float32) ** block_levels(arg_keys[9], (L * F,), ((0, 16),), -0.2, 0.2)), 4.0, 64.0).astype(jnp.bfloat16)
    same_first = centred(arg_keys[10], (L * F, D), 4.0, 24.0, ((0, 16), (1, 2)))
    same_second = jnp.clip(jnp.exp(math.log(64.0) - 2.7725887 * jax.random.uniform(arg_keys[11], (L * F, D), jnp.float32) ** block_levels(arg_keys[11], (L * F, D), ((0, 16), (1, 2)), -0.2, 0.2)), 4.0, 64.0).astype(jnp.bfloat16)
    next_first = centred(arg_keys[12], (F, D), 4.0, 24.0, ((0, 16), (1, 2)))
    next_second = jnp.clip(jnp.exp(math.log(64.0) - 2.7725887 * jax.random.uniform(arg_keys[13], (F, D), jnp.float32) ** block_levels(arg_keys[13], (F, D), ((0, 16), (1, 2)), -0.2, 0.2)), 4.0, 64.0).astype(jnp.bfloat16)
    return dict(residual=residual, targets=targets, encoder=encoder, biases=biases, same_decoder=same_decoder, next_decoder=next_decoder, encoder_first=encoder_first, encoder_second=encoder_second, biases_first=biases_first, biases_second=biases_second, same_first=same_first, same_second=same_second, next_first=next_first, next_second=next_second)


beta_one = 0.9
beta_two = 0.999
learn_rate = 0.002
adam_eps = 1e-08
weight_decay = 0.1

def adamw_update(parameter, first, second, gradient, decay_rate):
    first_new = beta_one * first.astype(jnp.float32) + (1.0 - beta_one) * gradient
    second_new = beta_two * second.astype(jnp.float32) + (1.0 - beta_two) * gradient * gradient
    first_hat = first_new / (1.0 - beta_one ** STEPS)
    second_hat = second_new / (1.0 - beta_two ** STEPS)
    weight = parameter.astype(jnp.float32)
    updated = weight - learn_rate * (first_hat / (jnp.sqrt(second_hat) + adam_eps) + decay_rate * weight)
    return (updated.astype(jnp.bfloat16), first_new.astype(jnp.bfloat16), second_new.astype(jnp.bfloat16))

def reorder(block, tokens_count):
    return block.reshape(tokens_count, F // FD, 2, FD // 2).transpose(0, 2, 1, 3).reshape(tokens_count, F)

def restore(block, tokens_count):
    return block.reshape(tokens_count, 2, F // FD, FD // 2).transpose(0, 2, 1, 3).reshape(tokens_count, F)

def reference(residual, targets, encoder, biases, same_decoder, next_decoder, encoder_first, encoder_second, biases_first, biases_second, same_first, same_second, next_first, next_second):
    preact_blocks = []
    for layer_index in range(L):
        block = jnp.dot(residual[layer_index], encoder[:, layer_index * F:(layer_index + 1) * F], preferred_element_type=jnp.float32)
        preact_blocks.append(block + biases[layer_index * F:(layer_index + 1) * F].astype(jnp.float32))
    preact = jnp.concatenate(preact_blocks, axis=1)
    active = jnp.maximum(preact, 0.0).astype(jnp.bfloat16)
    active_zero = active[:, :F]
    active_one = active[:, F:]
    cross_input = reorder(active_zero, TOK)
    recon_zero = jnp.dot(active_zero, same_decoder[:F], preferred_element_type=jnp.float32)
    recon_one = jnp.dot(active_one, same_decoder[F:], preferred_element_type=jnp.float32) + jnp.dot(cross_input, next_decoder, preferred_element_type=jnp.float32)
    recon = jnp.stack([recon_zero, recon_one])
    delta = (recon - targets.astype(jnp.float32)).astype(jnp.bfloat16)
    grad_same = jnp.concatenate([jnp.dot(active_zero.T, delta[0], preferred_element_type=jnp.float32), jnp.dot(active_one.T, delta[1], preferred_element_type=jnp.float32)], axis=0)
    grad_next = jnp.dot(cross_input.T, delta[1], preferred_element_type=jnp.float32)
    cross_grad = restore(jnp.dot(delta[1], next_decoder.T, preferred_element_type=jnp.float32), TOK)
    grad_zero = jnp.dot(delta[0], same_decoder[:F].T, preferred_element_type=jnp.float32) + cross_grad
    grad_one = jnp.dot(delta[1], same_decoder[F:].T, preferred_element_type=jnp.float32)
    act_grad = jnp.concatenate([grad_zero, grad_one], axis=1)
    preact_grad = jnp.where(preact > 0.0, act_grad, 0.0)
    grad_biases = lax.optimization_barrier(jnp.sum(preact_grad, axis=0))
    preact_low = preact_grad.astype(jnp.bfloat16)
    grad_encoder = jnp.concatenate([jnp.dot(residual[layer_index].T, preact_low[:, layer_index * F:(layer_index + 1) * F], preferred_element_type=jnp.float32) for layer_index in range(L)], axis=1)
    updated_encoder, encoder_moment, encoder_square = adamw_update(encoder, encoder_first, encoder_second, grad_encoder, weight_decay)
    updated_biases, biases_moment, biases_square = adamw_update(biases, biases_first, biases_second, grad_biases, 0.0)
    updated_same, same_moment, same_square = adamw_update(same_decoder, same_first, same_second, grad_same, weight_decay)
    updated_next, next_moment, next_square = adamw_update(next_decoder, next_first, next_second, grad_next, weight_decay)
    return (updated_encoder, updated_biases, updated_same, updated_next, encoder_moment, encoder_square, biases_moment, biases_square, same_moment, same_square, next_moment, next_square)
```

```python
import jax
import jax.numpy as jnp
from jax import lax
from jax.sharding import PartitionSpec as P

STEPS = 100


beta_one = 0.9
beta_two = 0.999
learn_rate = 0.002
adam_eps = 1e-08
weight_decay = 0.1


def adamw_update(parameter, first, second, gradient, decay_rate):
    first_new = beta_one * first.astype(jnp.float32) + (1.0 - beta_one) * gradient
    second_new = beta_two * second.astype(jnp.float32) + (1.0 - beta_two) * gradient * gradient
    first_hat = first_new / (1.0 - beta_one**STEPS)
    second_hat = second_new / (1.0 - beta_two**STEPS)
    weight = parameter.astype(jnp.float32)
    updated = weight - learn_rate * (
        first_hat / (jnp.sqrt(second_hat) + adam_eps) + decay_rate * weight
    )
    return (
        updated.astype(jnp.bfloat16),
        first_new.astype(jnp.bfloat16),
        second_new.astype(jnp.bfloat16),
    )


def matmul(left, right):
    return jnp.dot(left, right, preferred_element_type=jnp.float32)


def over_rows(left, right):
    return lax.dot_general(
        left, right, (((0,), (0,)), ((), ())), preferred_element_type=jnp.float32
    )


def over_cols(left, right):
    return lax.dot_general(
        left, right, (((1,), (1,)), ((), ())), preferred_element_type=jnp.float32
    )


def across(value):
    return lax.ppermute(value, "width", [(0, 1), (1, 0)])


def flipped(value, bit, members):
    step = 1 << bit
    return lax.ppermute(value, "feat", [(index, index ^ step) for index in range(members)])


def halves(value, axis):
    size = value.shape[axis] // 2
    return lax.slice_in_dim(value, 0, size, axis=axis), lax.slice_in_dim(
        value, size, 2 * size, axis=axis
    )


def scatter_step(total, bit, axis, members):
    upper = ((lax.axis_index("feat") >> bit) & 1) == 1
    low, high = halves(total, axis)
    leaving = jnp.where(upper, low, high).astype(jnp.bfloat16)
    keeping = jnp.where(upper, high, low)
    return keeping + flipped(leaving, bit, members).astype(jnp.float32)


def gather_step(value, bit, axis, members):
    upper = ((lax.axis_index("feat") >> bit) & 1) == 1
    other = flipped(value, bit, members)
    return jnp.concatenate(
        [jnp.where(upper, other, value), jnp.where(upper, value, other)], axis=axis
    )


def shard_of(target, plan, width_index):
    index = lax.axis_index("feat")
    starts, sizes = [0, 0], list(target.shape)
    for bit, axis in plan:
        sizes[axis] //= 2
        starts[axis] = starts[axis] + ((index >> bit) & 1) * sizes[axis]
    tokens = target.shape[0]
    starts[0] = lax.rem(starts[0] + width_index * (tokens // 2), tokens)
    return lax.dynamic_slice(target, starts, sizes)


def local(
    residual,
    targets,
    encoder,
    biases,
    same_decoder,
    next_decoder,
    encoder_first,
    encoder_second,
    biases_first,
    biases_second,
    same_first,
    same_second,
    next_first,
    next_second,
):
    feat_count = lax.axis_size("feat")
    feat_index = lax.axis_index("feat")
    width_index = lax.axis_index("width")
    half_count = feat_count // 2
    source_layer = feat_index // half_count
    leading = source_layer == 0
    tokens, width = residual.shape[1:]
    part = tokens // 2
    half = encoder.shape[1] // 2

    mine = lax.dynamic_slice(
        residual, (source_layer, width_index * part, 0), (1, part, width)
    )[0]
    theirs = lax.dynamic_slice(
        residual, (source_layer, (1 - width_index) * part, 0), (1, part, width)
    )[0]
    bias = biases.astype(jnp.float32)

    def preact_of(block, bias_block):
        leaving = matmul(theirs, block).astype(jnp.float16)
        arriving = across(leaving)
        return matmul(mine, block) + arriving.astype(jnp.float32) + bias_block

    pre_b = preact_of(encoder[:, half:], bias[half:])
    pre_a = preact_of(encoder[:, :half], bias[:half])
    act_b = jnp.maximum(pre_b, 0.0).astype(jnp.bfloat16)
    act_a = jnp.maximum(pre_a, 0.0).astype(jnp.bfloat16)
    sent = lax.ppermute(
        act_b, "feat", [(index, index + half_count) for index in range(half_count)]
    )
    trailing_pairs = [
        (2 * index + side, 2 * index + 1 - side)
        for index in range(half_count, feat_count)
        for side in range(2)
    ]
    full_b = jnp.concatenate([act_b, across(act_b)], axis=0)
    full_a = jnp.concatenate([act_a, across(act_a)], axis=0)
    sent_full = jnp.concatenate(
        [sent, lax.ppermute(sent, ("feat", "width"), trailing_pairs)], axis=0
    )
    active = jnp.concatenate([full_a, full_b], axis=1)
    cross_input = jnp.where(leading, full_a, sent_full)

    own_term = matmul(active, same_decoder)
    cross_term = matmul(cross_input, next_decoder)
    second_part = jnp.where(leading, cross_term, own_term + cross_term)

    bits = feat_count.bit_length() - 1
    second_plan = [(bit, 1 if bit == 2 else 0) for bit in range(bits)]
    first_order = [0, 2, 1] + list(range(3, bits - 1))
    first_plan = [(bit, 1 if place == 2 else 0) for place, bit in enumerate(first_order)]
    first_sum, second_sum = own_term, second_part
    for bit, axis in second_plan:
        second_sum = scatter_step(second_sum, bit, axis, feat_count)
    for bit, axis in first_plan:
        first_sum = scatter_step(first_sum, bit, axis, half_count)
    delta_first = (
        first_sum - shard_of(targets[0], first_plan, width_index).astype(jnp.float32)
    ).astype(jnp.bfloat16)
    delta_next = (
        second_sum - shard_of(targets[1], second_plan, width_index).astype(jnp.float32)
    ).astype(jnp.bfloat16)
    for bit, axis in reversed(second_plan):
        delta_next = gather_step(delta_next, bit, axis, feat_count)
    for bit, axis in reversed(first_plan):
        delta_first = gather_step(delta_first, bit, axis, half_count)
    delta_own = jnp.where(leading, delta_first, delta_next)

    cross_back = over_cols(delta_next, next_decoder)
    cross_arriving = lax.ppermute(
        cross_back[part:].astype(jnp.bfloat16), ("feat", "width"), trailing_pairs
    )
    cross_sum = (cross_back[:part] + cross_arriving.astype(jnp.float32)).astype(jnp.bfloat16)
    returned = lax.ppermute(
        cross_sum, "feat", [(index + half_count, index) for index in range(half_count)]
    ).astype(jnp.float32)
    back_a = over_cols(delta_own, same_decoder[:half]) + jnp.where(leading, cross_back, 0.0)
    back_b = over_cols(delta_own, same_decoder[half:])

    def preact_grad_of(back, pre, extra):
        arriving = across(back[part:].astype(jnp.bfloat16)).astype(jnp.float32)
        total = back[:part] + arriving
        if extra is not None:
            total = total + extra
        return jnp.where(pre > 0.0, total, 0.0).astype(jnp.bfloat16)

    grad_a = preact_grad_of(back_a, pre_a, None)
    grad_b = preact_grad_of(back_b, pre_b, returned)
    grad_mine = jnp.concatenate([grad_a, grad_b], axis=1)
    grad_theirs = jnp.concatenate([across(grad_a), across(grad_b)], axis=1)
    grad_sum = jnp.sum(grad_mine.astype(jnp.float32), axis=0)
    grad_biases = grad_sum + across(grad_sum)

    grad_same = over_rows(active, delta_own)
    grad_next = over_rows(cross_input, delta_next)
    grad_encoder = over_rows(
        jnp.concatenate([mine, theirs], axis=0),
        jnp.concatenate([grad_mine, grad_theirs], axis=0),
    )
    updated_encoder, encoder_moment, encoder_square = adamw_update(
        encoder, encoder_first, encoder_second, grad_encoder, weight_decay
    )
    updated_biases, biases_moment, biases_square = adamw_update(
        biases, biases_first, biases_second, grad_biases, 0.0
    )
    updated_same, same_moment, same_square = adamw_update(
        same_decoder, same_first, same_second, grad_same, weight_decay
    )
    updated_next, next_moment, next_square = adamw_update(
        next_decoder, next_first, next_second, grad_next, weight_decay
    )
    return (
        updated_encoder,
        updated_biases,
        updated_same,
        updated_next,
        encoder_moment,
        encoder_square,
        biases_moment,
        biases_square,
        same_moment,
        same_square,
        next_moment,
        next_square,
    )


def solution(mesh):
    in_specs = (
        P(None, None, "width"),
        P(None, None, "width"),
        P("width", "feat"),
        P("feat"),
        P("feat", "width"),
        P("feat", "width"),
        P("width", "feat"),
        P("width", "feat"),
        P("feat"),
        P("feat"),
        P("feat", "width"),
        P("feat", "width"),
        P("feat", "width"),
        P("feat", "width"),
    )
    out_specs = (
        P("width", "feat"),
        P("feat"),
        P("feat", "width"),
        P("feat", "width"),
        P("width", "feat"),
        P("width", "feat"),
        P("feat"),
        P("feat"),
        P("feat", "width"),
        P("feat", "width"),
        P("feat", "width"),
        P("feat", "width"),
    )
    return jax.shard_map(local, mesh=mesh, in_specs=in_specs, out_specs=out_specs, check_vma=False)
```

```python
import functools
import math
import jax
import jax.numpy as jnp
from jax import lax
from jax.experimental import pallas as pl
from jax.experimental.pallas import tpu as pltpu
from jax.sharding import PartitionSpec as P

STEPS = 100


beta_one = 0.9
beta_two = 0.999
learn_rate = 0.002
adam_eps = 1e-08
weight_decay = 0.1


def adamw_update(parameter, first, second, gradient, decay_rate):
    first_new = beta_one * first.astype(jnp.float32) + (1.0 - beta_one) * gradient
    second_new = beta_two * second.astype(jnp.float32) + (1.0 - beta_two) * gradient * gradient
    first_hat = first_new / (1.0 - beta_one**STEPS)
    second_hat = second_new / (1.0 - beta_two**STEPS)
    weight = parameter.astype(jnp.float32)
    updated = weight - learn_rate * (
        first_hat / (jnp.sqrt(second_hat) + adam_eps) + decay_rate * weight
    )
    return (
        updated.astype(jnp.bfloat16),
        first_new.astype(jnp.bfloat16),
        second_new.astype(jnp.bfloat16),
    )


def adamw_kernel(decay_rate, tile, *refs):
    left_ref, right_ref, weight_ref, first_ref, second_ref = refs[:5]
    updated_ref, moment_ref, square_ref = refs[5:]
    first_scale, second_scale = 1.0 - beta_one**STEPS, 1.0 - beta_two**STEPS
    keep = 1.0 - learn_rate * decay_rate
    rate = learn_rate * math.sqrt(second_scale) / first_scale
    shift = adam_eps * math.sqrt(second_scale)
    left = left_ref[...]
    for start in range(0, weight_ref.shape[1], tile):
        columns = slice(start, start + tile)
        gradient = over_rows(left, right_ref[:, columns])
        scaled = (1.0 - beta_one) * gradient
        first_new = beta_one * first_ref[:, columns].astype(jnp.float32) + scaled
        second_new = (
            beta_two * second_ref[:, columns].astype(jnp.float32)
            + ((1.0 - beta_two) * gradient) * gradient
        )
        root = second_new * lax.rsqrt(second_new)
        step = (rate * first_new) * pl.reciprocal(root + shift, approx=True)
        updated = keep * weight_ref[:, columns].astype(jnp.float32) - step
        updated_ref[:, columns] = updated.astype(jnp.bfloat16)
        moment_ref[:, columns] = first_new.astype(jnp.bfloat16)
        square_ref[:, columns] = second_new.astype(jnp.bfloat16)


def adamw_matmul(left, right, weight, first, second, decay_rate):
    tokens = left.shape[0]
    rows, width = weight.shape
    block = math.gcd(rows, 256)
    tile = math.gcd(width, 256)
    whole = pl.BlockSpec((tokens, width), lambda place: (0, 0))
    strip = pl.BlockSpec((block, width), lambda place: (place, 0))
    return pl.pallas_call(
        functools.partial(adamw_kernel, decay_rate, tile),
        grid=(rows // block,),
        in_specs=[
            pl.BlockSpec((tokens, block), lambda place: (0, place)),
            whole,
            strip,
            strip,
            strip,
        ],
        out_specs=[strip] * 3,
        out_shape=[jax.ShapeDtypeStruct((rows, width), jnp.bfloat16)] * 3,
        compiler_params=pltpu.CompilerParams(vmem_limit_bytes=40 * 2**20),
        cost_estimate=pl.CostEstimate(
            flops=2 * tokens * rows * width,
            bytes_accessed=12 * rows * width,
            transcendentals=2 * rows * width,
        ),
    )(left, right, weight, first, second)


def matmul(left, right):
    return jnp.dot(left, right, preferred_element_type=jnp.float32)


def over_rows(left, right):
    return lax.dot_general(
        left, right, (((0,), (0,)), ((), ())), preferred_element_type=jnp.float32
    )


def over_cols(left, right):
    return lax.dot_general(
        left, right, (((1,), (1,)), ((), ())), preferred_element_type=jnp.float32
    )


def across(value):
    return lax.ppermute(value, "width", [(0, 1), (1, 0)])


def flipped(value, bit, members):
    step = 1 << bit
    return lax.ppermute(value, "feat", [(index, index ^ step) for index in range(members)])


def halves(value, axis):
    size = value.shape[axis] // 2
    return lax.slice_in_dim(value, 0, size, axis=axis), lax.slice_in_dim(
        value, size, 2 * size, axis=axis
    )


def scatter_step(total, bit, axis, members):
    upper = ((lax.axis_index("feat") >> bit) & 1) == 1
    low, high = halves(total, axis)
    leaving = jnp.where(upper, low, high).astype(jnp.bfloat16)
    keeping = jnp.where(upper, high, low)
    return keeping + flipped(leaving, bit, members).astype(jnp.float32)


def gather_step(value, bit, axis, members):
    upper = ((lax.axis_index("feat") >> bit) & 1) == 1
    other = flipped(value, bit, members)
    return jnp.concatenate(
        [jnp.where(upper, other, value), jnp.where(upper, value, other)], axis=axis
    )


def shard_of(target, plan, width_index):
    index = lax.axis_index("feat")
    starts, sizes = [0, 0], list(target.shape)
    for bit, axis in plan:
        sizes[axis] //= 2
        starts[axis] = starts[axis] + ((index >> bit) & 1) * sizes[axis]
    tokens = target.shape[0]
    starts[0] = lax.rem(starts[0] + width_index * (tokens // 2), tokens)
    return lax.dynamic_slice(target, starts, sizes)


def local(
    residual,
    targets,
    encoder,
    biases,
    same_decoder,
    next_decoder,
    encoder_first,
    encoder_second,
    biases_first,
    biases_second,
    same_first,
    same_second,
    next_first,
    next_second,
):
    feat_count = lax.axis_size("feat")
    feat_index = lax.axis_index("feat")
    width_index = lax.axis_index("width")
    half_count = feat_count // 2
    source_layer = feat_index // half_count
    leading = source_layer == 0
    tokens, width = residual.shape[1:]
    part = tokens // 2
    half = encoder.shape[1] // 2

    mine = lax.dynamic_slice(
        residual, (source_layer, width_index * part, 0), (1, part, width)
    )[0]
    theirs = lax.dynamic_slice(
        residual, (source_layer, (1 - width_index) * part, 0), (1, part, width)
    )[0]
    bias = biases.astype(jnp.float32)

    def preact_of(block, bias_block):
        leaving = matmul(theirs, block).astype(jnp.float16)
        arriving = across(leaving)
        return matmul(mine, block) + arriving.astype(jnp.float32) + bias_block

    pre_b = preact_of(encoder[:, half:], bias[half:])
    pre_a = preact_of(encoder[:, :half], bias[:half])
    act_b = jnp.maximum(pre_b, 0.0).astype(jnp.bfloat16)
    act_a = jnp.maximum(pre_a, 0.0).astype(jnp.bfloat16)
    sent = lax.ppermute(
        act_b, "feat", [(index, index + half_count) for index in range(half_count)]
    )
    trailing_pairs = [
        (2 * index + side, 2 * index + 1 - side)
        for index in range(half_count, feat_count)
        for side in range(2)
    ]
    full_b = jnp.concatenate([act_b, across(act_b)], axis=0)
    full_a = jnp.concatenate([act_a, across(act_a)], axis=0)
    sent_full = jnp.concatenate(
        [sent, lax.ppermute(sent, ("feat", "width"), trailing_pairs)], axis=0
    )
    active = jnp.concatenate([full_a, full_b], axis=1)
    cross_input = jnp.where(leading, full_a, sent_full)

    own_term = matmul(active, same_decoder)
    cross_term = matmul(cross_input, next_decoder)
    second_part = jnp.where(leading, cross_term, own_term + cross_term)

    bits = feat_count.bit_length() - 1
    second_plan = [(bit, 1 if bit == 2 else 0) for bit in range(bits)]
    first_order = [0, 2, 1] + list(range(3, bits - 1))
    first_plan = [(bit, 1 if place == 2 else 0) for place, bit in enumerate(first_order)]
    first_sum, second_sum = own_term, second_part
    for bit, axis in second_plan:
        second_sum = scatter_step(second_sum, bit, axis, feat_count)
    for bit, axis in first_plan:
        first_sum = scatter_step(first_sum, bit, axis, half_count)
    delta_first = (
        first_sum - shard_of(targets[0], first_plan, width_index).astype(jnp.float32)
    ).astype(jnp.bfloat16)
    delta_next = (
        second_sum - shard_of(targets[1], second_plan, width_index).astype(jnp.float32)
    ).astype(jnp.bfloat16)
    for bit, axis in reversed(second_plan):
        delta_next = gather_step(delta_next, bit, axis, feat_count)
    for bit, axis in reversed(first_plan):
        delta_first = gather_step(delta_first, bit, axis, half_count)
    delta_own = jnp.where(leading, delta_first, delta_next)

    cross_back = over_cols(delta_next, next_decoder)
    cross_arriving = lax.ppermute(
        cross_back[part:].astype(jnp.bfloat16), ("feat", "width"), trailing_pairs
    )
    cross_sum = (cross_back[:part] + cross_arriving.astype(jnp.float32)).astype(jnp.bfloat16)
    returned = lax.ppermute(
        cross_sum, "feat", [(index + half_count, index) for index in range(half_count)]
    ).astype(jnp.float32)
    back_a = over_cols(delta_own, same_decoder[:half]) + jnp.where(leading, cross_back, 0.0)
    back_b = over_cols(delta_own, same_decoder[half:])

    def preact_grad_of(back, pre, extra):
        arriving = across(back[part:].astype(jnp.bfloat16)).astype(jnp.float32)
        total = back[:part] + arriving
        if extra is not None:
            total = total + extra
        return jnp.where(pre > 0.0, total, 0.0).astype(jnp.bfloat16)

    grad_a = preact_grad_of(back_a, pre_a, None)
    grad_b = preact_grad_of(back_b, pre_b, returned)
    grad_mine = jnp.concatenate([grad_a, grad_b], axis=1)
    grad_theirs = jnp.concatenate([across(grad_a), across(grad_b)], axis=1)
    grad_sum = jnp.sum(grad_mine.astype(jnp.float32), axis=0)
    grad_biases = grad_sum + across(grad_sum)

    updated_same, same_moment, same_square = adamw_matmul(
        active, delta_own, same_decoder, same_first, same_second, weight_decay
    )
    updated_next, next_moment, next_square = adamw_matmul(
        cross_input, delta_next, next_decoder, next_first, next_second, weight_decay
    )
    updated_encoder, encoder_moment, encoder_square = adamw_matmul(
        jnp.concatenate([mine, theirs], axis=0),
        jnp.concatenate([grad_mine, grad_theirs], axis=0),
        encoder,
        encoder_first,
        encoder_second,
        weight_decay,
    )
    updated_biases, biases_moment, biases_square = adamw_update(
        biases, biases_first, biases_second, grad_biases, 0.0
    )
    return (
        updated_encoder,
        updated_biases,
        updated_same,
        updated_next,
        encoder_moment,
        encoder_square,
        biases_moment,
        biases_square,
        same_moment,
        same_square,
        next_moment,
        next_square,
    )


def solution(mesh):
    in_specs = (
        P(None, None, "width"),
        P(None, None, "width"),
        P("width", "feat"),
        P("feat"),
        P("feat", "width"),
        P("feat", "width"),
        P("width", "feat"),
        P("width", "feat"),
        P("feat"),
        P("feat"),
        P("feat", "width"),
        P("feat", "width"),
        P("feat", "width"),
        P("feat", "width"),
    )
    out_specs = (
        P("width", "feat"),
        P("feat"),
        P("feat", "width"),
        P("feat", "width"),
        P("width", "feat"),
        P("width", "feat"),
        P("feat"),
        P("feat"),
        P("feat", "width"),
        P("feat", "width"),
        P("feat", "width"),
        P("feat", "width"),
    )
    return jax.shard_map(local, mesh=mesh, in_specs=in_specs, out_specs=out_specs, check_vma=False)
```

```python
import functools
import math
import jax
import jax.numpy as jnp
from jax import lax
from jax.experimental import pallas as pl
from jax.experimental.pallas import tpu as pltpu
from jax.sharding import PartitionSpec as P

STEPS = 100


beta_one = 0.9
beta_two = 0.999
learn_rate = 0.002
adam_eps = 1e-08
weight_decay = 0.1


def adamw_update(parameter, first, second, gradient, decay_rate):
    first_new = beta_one * first.astype(jnp.float32) + (1.0 - beta_one) * gradient
    second_new = beta_two * second.astype(jnp.float32) + (1.0 - beta_two) * gradient * gradient
    first_hat = first_new / (1.0 - beta_one**STEPS)
    second_hat = second_new / (1.0 - beta_two**STEPS)
    weight = parameter.astype(jnp.float32)
    updated = weight - learn_rate * (
        first_hat / (jnp.sqrt(second_hat) + adam_eps) + decay_rate * weight
    )
    return (
        updated.astype(jnp.bfloat16),
        first_new.astype(jnp.bfloat16),
        second_new.astype(jnp.bfloat16),
    )


def adamw_kernel(decay_rate, tile, pieces, *refs):
    left_refs, right_refs = refs[:pieces], refs[pieces : 2 * pieces]
    weight_ref, first_ref, second_ref = refs[2 * pieces : 2 * pieces + 3]
    updated_ref, moment_ref, square_ref = refs[-3:]
    first_scale, second_scale = 1.0 - beta_one**STEPS, 1.0 - beta_two**STEPS
    keep = 1.0 - learn_rate * decay_rate
    rate = learn_rate * math.sqrt(second_scale) / first_scale
    shift = adam_eps * math.sqrt(second_scale)
    for start in range(0, weight_ref.shape[1], tile):
        columns = slice(start, start + tile)
        gradient = over_rows(left_refs[0][...], right_refs[0][:, columns])
        for left_ref, right_ref in zip(left_refs[1:], right_refs[1:]):
            gradient = gradient + over_rows(left_ref[...], right_ref[:, columns])
        scaled = (1.0 - beta_one) * gradient
        first_new = beta_one * first_ref[:, columns].astype(jnp.float32) + scaled
        second_new = (
            beta_two * second_ref[:, columns].astype(jnp.float32)
            + ((1.0 - beta_two) * gradient) * gradient
        )
        root = second_new * lax.rsqrt(second_new)
        step = (rate * first_new) * pl.reciprocal(root + shift, approx=True)
        updated = keep * weight_ref[:, columns].astype(jnp.float32) - step
        updated_ref[:, columns] = updated.astype(jnp.bfloat16)
        moment_ref[:, columns] = first_new.astype(jnp.bfloat16)
        square_ref[:, columns] = second_new.astype(jnp.bfloat16)


def adamw_matmul(
    lefts, rights, weight, first, second, decay_rate, share=(0, 1), partly_done=()
):
    rows, width = weight.shape
    block = math.gcd(rows // share[1], 256)
    count = rows // share[1] // block
    base = share[0] * count
    tile = math.gcd(width, 256)
    strip = pl.BlockSpec((block, width), lambda place: (base + place, 0))
    left_specs = [
        pl.BlockSpec((left.shape[0], block), lambda place: (0, base + place)) for left in lefts
    ]
    right_specs = [pl.BlockSpec(right.shape, lambda place: (0, 0)) for right in rights]
    tokens = sum(left.shape[0] for left in lefts)
    return pl.pallas_call(
        functools.partial(adamw_kernel, decay_rate, tile, len(lefts)),
        grid=(count,),
        in_specs=left_specs
        + right_specs
        + [strip] * 3
        + [pl.BlockSpec(memory_space=pl.ANY)] * len(partly_done),
        out_specs=[strip] * 3,
        out_shape=[jax.ShapeDtypeStruct((rows, width), jnp.bfloat16)] * 3,
        input_output_aliases={2 * len(lefts) + 3 + at: at for at in range(len(partly_done))},
        compiler_params=pltpu.CompilerParams(vmem_limit_bytes=40 * 2**20),
        cost_estimate=pl.CostEstimate(
            flops=2 * tokens * block * count * width,
            bytes_accessed=12 * block * count * width,
            transcendentals=2 * block * count * width,
        ),
    )(*lefts, *rights, weight, first, second, *partly_done)


def matmul(left, right):
    return jnp.dot(left, right, preferred_element_type=jnp.float32)


def over_rows(left, right):
    return lax.dot_general(
        left, right, (((0,), (0,)), ((), ())), preferred_element_type=jnp.float32
    )


def over_cols(left, right):
    return lax.dot_general(
        left, right, (((1,), (1,)), ((), ())), preferred_element_type=jnp.float32
    )


def across(value):
    return lax.ppermute(value, "width", [(0, 1), (1, 0)])


def flipped(value, bit, members):
    step = 1 << bit
    return lax.ppermute(value, "feat", [(index, index ^ step) for index in range(members)])


def halves(value, axis):
    size = value.shape[axis] // 2
    return lax.slice_in_dim(value, 0, size, axis=axis), lax.slice_in_dim(
        value, size, 2 * size, axis=axis
    )


def is_upper(bit):
    return ((lax.axis_index("feat") >> bit) & 1) == 1


def split_for(total, bit, axis):
    low, high = halves(total, axis)
    upper = is_upper(bit)
    return jnp.where(upper, high, low), jnp.where(upper, low, high).astype(jnp.bfloat16)


def joined(own, other, bit, axis):
    upper = is_upper(bit)
    return jnp.concatenate(
        [jnp.where(upper, other, own), jnp.where(upper, own, other)], axis=axis
    )


def plan_of(order):
    last = len(order) - 1
    return [
        (bit, None if place == last else 1 if place == 2 else 0)
        for place, bit in enumerate(order)
    ]


def sent_block(total, step, members):
    bit, axis = step
    if axis is None:
        return total, flipped(total.astype(jnp.bfloat16), bit, members)
    keeping, leaving = split_for(total, bit, axis)
    return keeping, flipped(leaving, bit, members)


def ordered(*groups):
    return lax.optimization_barrier(groups)


class Order:
    def __init__(self, threads):
        self.threads = threads
        self.waiting = [next(thread)[1] for thread in threads]
        self.last = ()

    def advance(self, which):
        inputs, _ = ordered(self.waiting[which], self.last)
        self.last, self.waiting[which] = self.threads[which].send(inputs)

    def after(self, values):
        return ordered(values, self.last)[0]


def local(
    residual,
    targets,
    encoder,
    biases,
    same_decoder,
    next_decoder,
    encoder_first,
    encoder_second,
    biases_first,
    biases_second,
    same_first,
    same_second,
    next_first,
    next_second,
):
    feat_count = lax.axis_size("feat")
    feat_index = lax.axis_index("feat")
    width_index = lax.axis_index("width")
    half_count = feat_count // 2
    source_layer = feat_index // half_count
    leading = source_layer == 0
    tokens, width = residual.shape[1:]
    chunks = 2
    part = tokens // (2 * chunks)
    half = encoder.shape[1] // 2
    bias = biases.astype(jnp.float32)
    downward = [(index, index + half_count) for index in range(half_count)]
    upward = [(index + half_count, index) for index in range(half_count)]
    trailing_pairs = [
        (2 * index + side, 2 * index + 1 - side)
        for index in range(half_count, feat_count)
        for side in range(2)
    ]

    def rows_of(chunk):
        blocks = [
            lax.dynamic_slice(
                residual,
                (source_layer, side * (tokens // 2) + chunk * part, 0),
                (1, part, width),
            )
            for side in (width_index, 1 - width_index)
        ]
        return jnp.concatenate(blocks, axis=1)[0]

    def wanted_block(layer, chunk, plan):
        starts, sizes = [0, 0], [2 * part, width]
        for bit, axis in plan:
            if axis is not None:
                sizes[axis] //= 2
                starts[axis] = starts[axis] + is_upper(bit).astype(jnp.int32) * sizes[axis]
        side = jnp.where(starts[0] >= part, 1 - width_index, width_index)
        row = side * (tokens // 2) + chunk * part + lax.rem(starts[0], part)
        block = lax.dynamic_slice(targets, (layer, row, starts[1]), (1, *sizes))
        return block[0].astype(jnp.float32)

    inputs = [rows_of(chunk) for chunk in range(chunks)]
    bits = feat_count.bit_length() - 1
    second_plan = plan_of(list(range(bits)))
    first_plan = plan_of([0, 2, 1] + list(range(3, bits - 1)))
    def add(total, arrived):
        return total + arrived.astype(jnp.float32)

    def stages_of(layer, plan):
        moves = [("sum", *step) for step in plan[1:]]
        backward = [("join", *step) for step in reversed(plan[1:]) if step[1] is not None]
        return [(layer, plan, move) for move in moves + backward]

    stages = [stages_of(0, first_plan), stages_of(1, second_plan)]
    members = [half_count, feat_count]

    def settle(layer, place, chunk, value, other):
        if place > len(stages[layer]):
            return value
        before = stages[layer][place - 1][2] if place > 0 else ("sum",)
        last_sum = len([0 for stage in stages[layer] if stage[2][0] == "sum"])
        if before[0] == "sum":
            value = add(value, other)
            if place == last_sum:
                plan = (first_plan, second_plan)[layer]
                value = (value - wanted_block(layer, chunk, plan)).astype(jnp.bfloat16)
            return value
        return joined(value, other, *before[1:])

    def move(layer, place, value):
        if place >= len(stages[layer]):
            return value, value
        kind, bit, axis = stages[layer][place][2]
        if kind == "sum":
            return sent_block(value, (bit, axis), members[layer])
        return value, flipped(value, bit, members[layer])

    def chunk_steps(chunk):
        (given,) = yield (), (inputs[chunk],)
        partial_pre = matmul(given, encoder)
        leaving = partial_pre[part:].astype(jnp.float16)
        keeping, arriving = yield (leaving,), (partial_pre[:part], across(leaving))
        pre = add(keeping, arriving) + bias
        shared = jnp.maximum(pre, 0.0).astype(jnp.bfloat16)
        sent = lax.ppermute(shared[:, half:], "feat", downward)
        shared, other, sent = yield (shared,), (shared, across(shared), sent)
        sent_other = lax.ppermute(sent, ("feat", "width"), trailing_pairs)
        active = jnp.concatenate([shared, other], axis=0)
        own_term = matmul(active, same_decoder)
        sent, sent_other, own_term = yield (own_term,), (sent, sent_other, own_term)
        sent_full = jnp.concatenate([sent, sent_other], axis=0)
        cross_input = jnp.where(leading, active[:, :half], sent_full)
        cross_term = matmul(cross_input, next_decoder)
        second_part = jnp.where(leading, cross_term, own_term + cross_term)
        values, leaves = zip(*[split_for(own_term, 0, 0), split_for(second_part, 0, 0)])
        leaving = jnp.concatenate(leaves, axis=0)
        values, arriving = yield (leaving,), (values, flipped(leaving, 0, feat_count))
        others = halves(arriving, 0)
        for place in range(len(stages[1])):
            values = [settle(layer, place, chunk, values[layer], others[layer]) for layer in (0, 1)]
            values, others = zip(*[move(layer, place, values[layer]) for layer in (0, 1)])
            values, others = yield values, (values, others)
        place = len(stages[1])
        values = [settle(layer, place, chunk, values[layer], others[layer]) for layer in (0, 1)]
        both = jnp.concatenate(values, axis=0)
        values, arriving = yield (both,), (values, flipped(both, 0, feat_count))
        others = halves(arriving, 0)
        delta_first, delta_next = [joined(values[layer], others[layer], 0, 0) for layer in (0, 1)]
        delta_own = jnp.where(leading, delta_first, delta_next)
        cross_back = over_cols(delta_next, next_decoder)
        cross_leaving = cross_back[part:].astype(jnp.bfloat16)
        cross_arriving = lax.ppermute(cross_leaving, ("feat", "width"), trailing_pairs)
        back = over_cols(delta_own, same_decoder)
        back_a = back[:, :half] + jnp.where(leading, cross_back, 0.0)
        back = jnp.concatenate([back_a, back[:, half:]], axis=1)
        leaving = back[part:].astype(jnp.bfloat16)
        arriving = across(leaving)
        grads[chunk] = (active, delta_own, cross_input, delta_next)
        cross_keeping, cross_arriving = yield (leaving,), (cross_back[:part], cross_arriving)
        cross_sum = add(cross_keeping, cross_arriving).astype(jnp.bfloat16)
        returned = lax.ppermute(cross_sum, "feat", upward)
        keeping, arriving, returned = yield (cross_sum,), (back[:part], arriving, returned)
        total = add(keeping, arriving)
        total = jnp.concatenate([total[:, :half], add(total[:, half:], returned)], axis=1)
        shared = jnp.where(pre > 0.0, total, 0.0).astype(jnp.bfloat16)
        sums[chunk] = jnp.sum(shared.astype(jnp.float32), axis=0)
        shared, other = yield (shared,), (shared, across(shared))
        preact_grad[chunk] = jnp.concatenate([shared, other], axis=0)
        yield (preact_grad[chunk],), ()

    grads, sums, preact_grad = {}, {}, {}
    order = Order([chunk_steps(0), chunk_steps(1)])
    steps = len(stages[1]) + 9
    turns = [0, 0, 1, 0, 0, 1, 0, 0, 1, 0, 0, 1]
    turns += [0, 1] * (steps - turns.count(0))
    for which in turns:
        order.advance(which)
    for _ in range(steps - 3 - turns.count(1)):
        order.advance(1)

    active, delta_own, cross_input, delta_next = zip(grads[0], grads[1])
    next_done = adamw_matmul(
        cross_input, delta_next, next_decoder, next_first, next_second, weight_decay
    )
    order.last = next_done
    order.advance(1)
    same_done = adamw_matmul(
        active, order.after(delta_own), same_decoder, same_first, same_second, weight_decay, (0, 2)
    )
    order.last = same_done
    order.advance(1)
    same_done = adamw_matmul(
        active,
        order.after(delta_own),
        same_decoder,
        same_first,
        same_second,
        weight_decay,
        (1, 2),
        same_done,
    )
    order.last = same_done
    order.advance(1)
    grad_sum = sums[0] + sums[1]
    grad_biases = grad_sum + across(grad_sum)
    updated_same, same_moment, same_square = same_done
    updated_next, next_moment, next_square = next_done
    updated_encoder, encoder_moment, encoder_square = adamw_matmul(
        inputs,
        (preact_grad[0], preact_grad[1]),
        encoder,
        encoder_first,
        encoder_second,
        weight_decay,
    )
    updated_biases, biases_moment, biases_square = adamw_update(
        biases, biases_first, biases_second, grad_biases, 0.0
    )
    return (
        updated_encoder,
        updated_biases,
        updated_same,
        updated_next,
        encoder_moment,
        encoder_square,
        biases_moment,
        biases_square,
        same_moment,
        same_square,
        next_moment,
        next_square,
    )


def solution(mesh):
    in_specs = (
        P(None, None, "width"),
        P(None, None, "width"),
        P("width", "feat"),
        P("feat"),
        P("feat", "width"),
        P("feat", "width"),
        P("width", "feat"),
        P("width", "feat"),
        P("feat"),
        P("feat"),
        P("feat", "width"),
        P("feat", "width"),
        P("feat", "width"),
        P("feat", "width"),
    )
    out_specs = (
        P("width", "feat"),
        P("feat"),
        P("feat", "width"),
        P("feat", "width"),
        P("width", "feat"),
        P("width", "feat"),
        P("feat"),
        P("feat"),
        P("feat", "width"),
        P("feat", "width"),
        P("feat", "width"),
        P("feat", "width"),
    )
    return jax.shard_map(local, mesh=mesh, in_specs=in_specs, out_specs=out_specs, check_vma=False)
```

```python
import functools
import math
import jax
import jax.numpy as jnp
from jax import lax
from jax.experimental import pallas as pl
from jax.experimental.pallas import tpu as pltpu
from jax.sharding import PartitionSpec as P

STEPS = 100


beta_one = 0.9
beta_two = 0.999
learn_rate = 0.002
adam_eps = 1e-08
weight_decay = 0.1


def adamw_update(parameter, first, second, gradient, decay_rate):
    first_new = beta_one * first.astype(jnp.float32) + (1.0 - beta_one) * gradient
    second_new = beta_two * second.astype(jnp.float32) + (1.0 - beta_two) * gradient * gradient
    first_hat = first_new / (1.0 - beta_one**STEPS)
    second_hat = second_new / (1.0 - beta_two**STEPS)
    weight = parameter.astype(jnp.float32)
    updated = weight - learn_rate * (
        first_hat / (jnp.sqrt(second_hat) + adam_eps) + decay_rate * weight
    )
    return (
        updated.astype(jnp.bfloat16),
        first_new.astype(jnp.bfloat16),
        second_new.astype(jnp.bfloat16),
    )


def adamw_kernel(decay_rate, tile, *refs):
    left_ref, right_ref, weight_ref, first_ref, second_ref = refs[:5]
    updated_ref, moment_ref, square_ref = refs[-3:]
    first_scale, second_scale = 1.0 - beta_one**STEPS, 1.0 - beta_two**STEPS
    keep = 1.0 - learn_rate * decay_rate
    rate = learn_rate * math.sqrt(second_scale) / first_scale
    shift = adam_eps * math.sqrt(second_scale)
    for start in range(0, weight_ref.shape[1], tile):
        columns = slice(start, start + tile)
        gradient = over_rows(left_ref[...], right_ref[:, columns])
        scaled = (1.0 - beta_one) * gradient
        first_new = beta_one * first_ref[:, columns].astype(jnp.float32) + scaled
        second_new = (
            beta_two * second_ref[:, columns].astype(jnp.float32)
            + ((1.0 - beta_two) * gradient) * gradient
        )
        root = second_new * lax.rsqrt(second_new)
        step = (rate * first_new) * pl.reciprocal(root + shift, approx=True)
        updated = keep * weight_ref[:, columns].astype(jnp.float32) - step
        updated_ref[:, columns] = updated.astype(jnp.bfloat16)
        moment_ref[:, columns] = first_new.astype(jnp.bfloat16)
        square_ref[:, columns] = second_new.astype(jnp.bfloat16)


def adamw_matmul(left, right, weight, first, second, decay_rate, share=(0, 1), partly_done=()):
    tokens = left.shape[0]
    rows, width = weight.shape
    block = math.gcd(rows, 256)
    span = width // share[1]
    tile = math.gcd(span, 256)
    strip = pl.BlockSpec((block, span), lambda place: (place, share[0]))
    return pl.pallas_call(
        functools.partial(adamw_kernel, decay_rate, tile),
        grid=(rows // block,),
        in_specs=[
            pl.BlockSpec((tokens, block), lambda place: (0, place)),
            pl.BlockSpec((tokens, span), lambda place: (0, 0)),
            strip,
            strip,
            strip,
        ]
        + [pl.BlockSpec(memory_space=pl.ANY)] * len(partly_done),
        out_specs=[strip] * 3,
        out_shape=[jax.ShapeDtypeStruct((rows, width), jnp.bfloat16)] * 3,
        input_output_aliases={5 + at: at for at in range(len(partly_done))},
        compiler_params=pltpu.CompilerParams(vmem_limit_bytes=40 * 2**20),
        cost_estimate=pl.CostEstimate(
            flops=2 * tokens * rows * span,
            bytes_accessed=12 * rows * span,
            transcendentals=2 * rows * span,
        ),
    )(left, right, weight, first, second, *partly_done)


def matmul(left, right):
    return jnp.dot(left, right, preferred_element_type=jnp.float32)


def over_rows(left, right):
    return lax.dot_general(
        left, right, (((0,), (0,)), ((), ())), preferred_element_type=jnp.float32
    )


def over_cols(left, right):
    return lax.dot_general(
        left, right, (((1,), (1,)), ((), ())), preferred_element_type=jnp.float32
    )


def across(value):
    return lax.ppermute(value, "width", [(0, 1), (1, 0)])


def flipped(value, bit, members):
    step = 1 << bit
    return lax.ppermute(value, "feat", [(index, index ^ step) for index in range(members)])


def halves(value, axis):
    size = value.shape[axis] // 2
    return lax.slice_in_dim(value, 0, size, axis=axis), lax.slice_in_dim(
        value, size, 2 * size, axis=axis
    )


def is_upper(bit):
    return ((lax.axis_index("feat") >> bit) & 1) == 1


def split_for(total, bit, axis):
    low, high = halves(total, axis)
    upper = is_upper(bit)
    return jnp.where(upper, high, low), jnp.where(upper, low, high).astype(jnp.bfloat16)


def joined(own, other, bit, axis):
    upper = is_upper(bit)
    return jnp.concatenate(
        [jnp.where(upper, other, own), jnp.where(upper, own, other)], axis=axis
    )


def plan_of(order):
    last = len(order) - 1
    return [
        (bit, None if place == last else 1 if place == 2 else 0)
        for place, bit in enumerate(order)
    ]


def add(total, arrived):
    return total + arrived.astype(jnp.float32)


def summed_steps(total, plan, members, wanted):
    for bit, axis in plan:
        if axis is None:
            keeping, leaving = total, total.astype(jnp.bfloat16)
        else:
            keeping, leaving = split_for(total, bit, axis)
        keeping, arrived = yield (leaving,), (keeping, flipped(leaving, bit, members))
        total = add(keeping, arrived)
    value = (total - wanted).astype(jnp.bfloat16)
    for bit, axis in reversed(plan):
        if axis is not None:
            value, other = yield (value,), (value, flipped(value, bit, members))
            value = joined(value, other, bit, axis)
    yield (value,), value


class Order:
    def __init__(self):
        self.last = ()
        self.waiting = {}

    def after(self, values):
        return lax.optimization_barrier((values, self.last))[0]

    def mark(self, *values):
        self.last = values

    def start(self, name, thread):
        self.last, pending = next(thread)
        self.waiting[name] = (thread, pending)

    def advance(self, name):
        thread, pending = self.waiting[name]
        self.last, pending = thread.send(self.after(pending))
        self.waiting[name] = (thread, pending)

    def result(self, name):
        return self.waiting[name][1]


def local(
    residual,
    targets,
    encoder,
    biases,
    same_decoder,
    next_decoder,
    encoder_first,
    encoder_second,
    biases_first,
    biases_second,
    same_first,
    same_second,
    next_first,
    next_second,
):
    feat_count = lax.axis_size("feat")
    feat_index = lax.axis_index("feat")
    width_index = lax.axis_index("width")
    half_count = feat_count // 2
    source_layer = feat_index // half_count
    leading = source_layer == 0
    tokens, width = residual.shape[1:]
    part = tokens // 2
    half = encoder.shape[1] // 2
    bias = biases.astype(jnp.float32)
    downward = [(index, index + half_count) for index in range(half_count)]
    upward = [(index + half_count, index) for index in range(half_count)]
    trailing_pairs = [
        (2 * index + side, 2 * index + 1 - side)
        for index in range(half_count, feat_count)
        for side in range(2)
    ]

    def wanted_block(layer, plan):
        starts, sizes = [0, 0], [tokens, width]
        for bit, axis in plan:
            if axis is not None:
                sizes[axis] //= 2
                starts[axis] = starts[axis] + is_upper(bit).astype(jnp.int32) * sizes[axis]
        row = lax.rem(starts[0] + width_index * part, tokens)
        block = lax.dynamic_slice(targets, (layer, row, starts[1]), (1, *sizes))
        return block[0].astype(jnp.float32)

    bits = feat_count.bit_length() - 1
    second_plan = plan_of(list(range(bits)))
    first_plan = plan_of(list(range(bits - 1)))
    order = Order()

    inputs = jnp.concatenate(
        [
            lax.dynamic_slice(residual, (source_layer, side * part, 0), (1, part, width))[0]
            for side in (width_index, 1 - width_index)
        ],
        axis=0,
    )
    partial_b = matmul(inputs, encoder[:, half:])
    leaving_b = partial_b[part:].astype(jnp.float16)
    arriving_b = across(leaving_b)
    leaving_a = matmul(inputs[part:], encoder[:, :half]).astype(jnp.float16)
    arriving_a = across(leaving_a)
    pre_b = add(partial_b[:part], arriving_b) + bias[half:]
    act_b = jnp.maximum(pre_b, 0.0).astype(jnp.bfloat16)
    sent = lax.ppermute(act_b, "feat", downward)
    sent_other = lax.ppermute(sent, ("feat", "width"), trailing_pairs)
    other_b = across(act_b)
    pre_a = add(matmul(inputs[:part], encoder[:, :half]), arriving_a) + bias[:half]
    act_a = jnp.maximum(pre_a, 0.0).astype(jnp.bfloat16)
    other_a = across(act_a)
    _, act_a, other_a = lax.optimization_barrier((sent, act_a, other_a))
    active = jnp.concatenate(
        [jnp.concatenate([act_a, act_b], axis=1), jnp.concatenate([other_a, other_b], axis=1)],
        axis=0,
    )
    own_term = matmul(active, same_decoder)
    order.start(
        0, summed_steps(own_term, first_plan, half_count, wanted_block(0, first_plan))
    )
    sent_other, own_term, sent = order.after((sent_other, own_term, sent))
    cross_input = jnp.where(leading, active[:, :half], jnp.concatenate([sent, sent_other], axis=0))
    cross_term = matmul(cross_input, next_decoder)
    second_part = jnp.where(leading, cross_term, own_term + cross_term)
    order.start(
        1, summed_steps(second_part, second_plan, feat_count, wanted_block(1, second_plan))
    )
    left = [len(plan) + len(plan) - 1 for plan in (first_plan, second_plan)]
    while left[1] > 0:
        for layer in (0, 1):
            if left[layer] > 0:
                order.advance(layer)
                left[layer] -= 1
    delta_first, delta_next = order.result(0), order.result(1)
    delta_own = jnp.where(leading, delta_first, delta_next)

    cross_back = over_cols(delta_next, next_decoder)
    cross_leaving = cross_back[part:].astype(jnp.bfloat16)
    cross_arriving = lax.ppermute(cross_leaving, ("feat", "width"), trailing_pairs)
    order.mark(cross_leaving)
    delta_own, cross_back = order.after((delta_own, cross_back))
    back_a = over_cols(delta_own, same_decoder[:half]) + jnp.where(leading, cross_back, 0.0)
    back_leaving = back_a[part:].astype(jnp.bfloat16)
    arriving_a = across(back_leaving)
    order.mark(back_leaving)
    delta_own, back_a = order.after((delta_own, back_a))
    back_b = over_cols(delta_own, same_decoder[half:])
    back_leaving = back_b[part:].astype(jnp.bfloat16)
    arriving_b = across(back_leaving)
    order.mark(back_leaving)
    next_done = adamw_matmul(
        order.after(cross_input), delta_next, next_decoder, next_first, next_second, weight_decay
    )
    order.mark(*next_done)
    kept_cross, cross_arriving = order.after((cross_back[:part], cross_arriving))
    cross_sum = add(kept_cross, cross_arriving).astype(jnp.bfloat16)
    returned = lax.ppermute(cross_sum, "feat", upward)
    order.mark(cross_sum)
    kept_a, arriving_a, pre_a = order.after((back_a[:part], arriving_a, pre_a))
    grad_a = jnp.where(pre_a > 0.0, add(kept_a, arriving_a), 0.0).astype(jnp.bfloat16)
    grad_other_a = across(grad_a)
    order.mark(grad_a)
    same_done = adamw_matmul(
        order.after(active), delta_own, same_decoder, same_first, same_second, weight_decay
    )
    order.mark(*same_done)
    kept_b, arriving_b, returned, pre_b = order.after((back_b[:part], arriving_b, returned, pre_b))
    total_b = add(add(kept_b, arriving_b), returned)
    grad_b = jnp.where(pre_b > 0.0, total_b, 0.0).astype(jnp.bfloat16)
    grad_other_b = across(grad_b)
    grad_sum = jnp.concatenate(
        [jnp.sum(grad.astype(jnp.float32), axis=0) for grad in (grad_a, grad_b)]
    )
    sum_other = across(grad_sum)
    order.mark(grad_b, grad_sum)
    grad_a, grad_other_a = order.after((grad_a, grad_other_a))
    encoder_done = adamw_matmul(
        inputs,
        jnp.concatenate([grad_a, grad_other_a], axis=0),
        encoder,
        encoder_first,
        encoder_second,
        weight_decay,
        (0, 2),
    )
    order.mark(*encoder_done)
    grad_b, grad_other_b, sum_other = order.after((grad_b, grad_other_b, sum_other))
    encoder_done = adamw_matmul(
        inputs,
        jnp.concatenate([grad_b, grad_other_b], axis=0),
        encoder,
        encoder_first,
        encoder_second,
        weight_decay,
        (1, 2),
        encoder_done,
    )
    grad_biases = grad_sum + sum_other
    updated_same, same_moment, same_square = same_done
    updated_next, next_moment, next_square = next_done
    updated_encoder, encoder_moment, encoder_square = encoder_done
    updated_biases, biases_moment, biases_square = adamw_update(
        biases, biases_first, biases_second, grad_biases, 0.0
    )
    return (
        updated_encoder,
        updated_biases,
        updated_same,
        updated_next,
        encoder_moment,
        encoder_square,
        biases_moment,
        biases_square,
        same_moment,
        same_square,
        next_moment,
        next_square,
    )


def solution(mesh):
    in_specs = (
        P(None, None, "width"),
        P(None, None, "width"),
        P("width", "feat"),
        P("feat"),
        P("feat", "width"),
        P("feat", "width"),
        P("width", "feat"),
        P("width", "feat"),
        P("feat"),
        P("feat"),
        P("feat", "width"),
        P("feat", "width"),
        P("feat", "width"),
        P("feat", "width"),
    )
    out_specs = (
        P("width", "feat"),
        P("feat"),
        P("feat", "width"),
        P("feat", "width"),
        P("width", "feat"),
        P("width", "feat"),
        P("feat"),
        P("feat"),
        P("feat", "width"),
        P("feat", "width"),
        P("feat", "width"),
        P("feat", "width"),
    )
    return jax.shard_map(local, mesh=mesh, in_specs=in_specs, out_specs=out_specs, check_vma=False)
```

```python
import functools
import math
import jax
import jax.numpy as jnp
from jax import lax
from jax.experimental import pallas as pl
from jax.experimental.pallas import tpu as pltpu
from jax.sharding import PartitionSpec as P

STEPS = 100


beta_one = 0.9
beta_two = 0.999
learn_rate = 0.002
adam_eps = 1e-08
weight_decay = 0.1


def adamw_update(parameter, first, second, gradient, decay_rate):
    first_new = beta_one * first.astype(jnp.float32) + (1.0 - beta_one) * gradient
    second_new = beta_two * second.astype(jnp.float32) + (1.0 - beta_two) * gradient * gradient
    first_hat = first_new / (1.0 - beta_one**STEPS)
    second_hat = second_new / (1.0 - beta_two**STEPS)
    weight = parameter.astype(jnp.float32)
    updated = weight - learn_rate * (
        first_hat / (jnp.sqrt(second_hat) + adam_eps) + decay_rate * weight
    )
    return (
        updated.astype(jnp.bfloat16),
        first_new.astype(jnp.bfloat16),
        second_new.astype(jnp.bfloat16),
    )


def adamw_kernel(decay_rate, tile, *refs):
    left_ref, right_ref, weight_ref, first_ref, second_ref = refs[:5]
    updated_ref, moment_ref, square_ref = refs[-3:]
    first_scale, second_scale = 1.0 - beta_one**STEPS, 1.0 - beta_two**STEPS
    keep = 1.0 - learn_rate * decay_rate
    rate = learn_rate * math.sqrt(second_scale) / first_scale
    shift = adam_eps * math.sqrt(second_scale)
    for start in range(0, weight_ref.shape[1], tile):
        columns = slice(start, start + tile)
        gradient = over_rows(left_ref[...], right_ref[:, columns])
        scaled = (1.0 - beta_one) * gradient
        first_new = beta_one * first_ref[:, columns].astype(jnp.float32) + scaled
        second_new = (
            beta_two * second_ref[:, columns].astype(jnp.float32)
            + ((1.0 - beta_two) * gradient) * gradient
        )
        root = second_new * lax.rsqrt(second_new)
        step = (rate * first_new) * pl.reciprocal(root + shift, approx=True)
        updated = keep * weight_ref[:, columns].astype(jnp.float32) - step
        updated_ref[:, columns] = updated.astype(jnp.bfloat16)
        moment_ref[:, columns] = first_new.astype(jnp.bfloat16)
        square_ref[:, columns] = second_new.astype(jnp.bfloat16)


def adamw_matmul(left, right, weight, first, second, decay_rate, share=(0, 1), partly_done=()):
    tokens = left.shape[0]
    rows, width = weight.shape
    span = width // share[1]
    block = math.gcd(rows, 256 if span <= 1024 else 128)
    tile = math.gcd(span, 256)
    strip = pl.BlockSpec((block, span), lambda place: (place, share[0]))
    return pl.pallas_call(
        functools.partial(adamw_kernel, decay_rate, tile),
        grid=(rows // block,),
        in_specs=[
            pl.BlockSpec((tokens, block), lambda place: (0, place)),
            pl.BlockSpec((tokens, span), lambda place: (0, 0), pipeline_mode=pl.Buffered(1)),
            strip,
            strip,
            strip,
        ]
        + [pl.BlockSpec(memory_space=pl.ANY)] * len(partly_done),
        out_specs=[strip] * 3,
        out_shape=[jax.ShapeDtypeStruct((rows, width), jnp.bfloat16)] * 3,
        input_output_aliases={5 + at: at for at in range(len(partly_done))},
        compiler_params=pltpu.CompilerParams(vmem_limit_bytes=14 * 2**20),
        cost_estimate=pl.CostEstimate(
            flops=2 * tokens * rows * span,
            bytes_accessed=12 * rows * span,
            transcendentals=2 * rows * span,
        ),
    )(left, right, weight, first, second, *partly_done)


def matmul(left, right):
    return jnp.dot(left, right, preferred_element_type=jnp.float32)


def over_rows(left, right):
    return lax.dot_general(
        left, right, (((0,), (0,)), ((), ())), preferred_element_type=jnp.float32
    )


def over_cols(left, right):
    return lax.dot_general(
        left, right, (((1,), (1,)), ((), ())), preferred_element_type=jnp.float32
    )


def across(value):
    return lax.ppermute(value, "width", [(0, 1), (1, 0)])


def flipped(value, bit, members):
    step = 1 << bit
    return lax.ppermute(value, "feat", [(index, index ^ step) for index in range(members)])


def halves(value, axis):
    size = value.shape[axis] // 2
    return lax.slice_in_dim(value, 0, size, axis=axis), lax.slice_in_dim(
        value, size, 2 * size, axis=axis
    )


def is_upper(bit):
    return ((lax.axis_index("feat") >> bit) & 1) == 1


def split_for(total, bit, axis):
    low, high = halves(total, axis)
    upper = is_upper(bit)
    return jnp.where(upper, high, low), jnp.where(upper, low, high).astype(jnp.bfloat16)


def joined(own, other, bit, axis):
    upper = is_upper(bit)
    return jnp.concatenate(
        [jnp.where(upper, other, own), jnp.where(upper, own, other)], axis=axis
    )


def plan_of(order):
    last = len(order) - 1
    return [
        (bit, None if place == last else 1 if place == 2 else 0)
        for place, bit in enumerate(order)
    ]


def add(total, arrived):
    return total + arrived.astype(jnp.float32)


def summed_steps(total, plan, members, wanted):
    for bit, axis in plan:
        if axis is None:
            keeping, leaving = total, total.astype(jnp.bfloat16)
        else:
            keeping, leaving = split_for(total, bit, axis)
        keeping, arrived = yield (leaving,), (keeping, flipped(leaving, bit, members))
        total = add(keeping, arrived)
    value = (total - wanted).astype(jnp.bfloat16)
    for bit, axis in reversed(plan):
        if axis is not None:
            value, other = yield (value,), (value, flipped(value, bit, members))
            value = joined(value, other, bit, axis)
    yield (value,), value


class Order:
    def __init__(self):
        self.last = ()
        self.waiting = {}

    def after(self, values):
        return lax.optimization_barrier((values, self.last))[0]

    def mark(self, *values):
        self.last = values

    def start(self, name, thread):
        self.last, pending = next(thread)
        self.waiting[name] = (thread, pending)

    def advance(self, name):
        thread, pending = self.waiting[name]
        self.last, pending = thread.send(self.after(pending))
        self.waiting[name] = (thread, pending)

    def result(self, name):
        return self.waiting[name][1]


def local(
    residual,
    targets,
    encoder,
    biases,
    same_decoder,
    next_decoder,
    encoder_first,
    encoder_second,
    biases_first,
    biases_second,
    same_first,
    same_second,
    next_first,
    next_second,
):
    feat_count = lax.axis_size("feat")
    feat_index = lax.axis_index("feat")
    width_index = lax.axis_index("width")
    half_count = feat_count // 2
    source_layer = feat_index // half_count
    leading = source_layer == 0
    tokens, width = residual.shape[1:]
    part = tokens // 2
    half = encoder.shape[1] // 2
    bias = biases.astype(jnp.float32)
    downward = [(index, index + half_count) for index in range(half_count)]
    upward = [(index + half_count, index) for index in range(half_count)]
    trailing_pairs = [
        (2 * index + side, 2 * index + 1 - side)
        for index in range(half_count, feat_count)
        for side in range(2)
    ]

    def wanted_block(layer, plan):
        starts, sizes = [0, 0], [tokens, width]
        for bit, axis in plan:
            if axis is not None:
                sizes[axis] //= 2
                starts[axis] = starts[axis] + is_upper(bit).astype(jnp.int32) * sizes[axis]
        row = lax.rem(starts[0] + width_index * part, tokens)
        block = lax.dynamic_slice(targets, (layer, row, starts[1]), (1, *sizes))
        return block[0].astype(jnp.float32)

    bits = feat_count.bit_length() - 1
    second_plan = plan_of(list(range(bits)))
    first_plan = plan_of(list(range(bits - 1)))
    order = Order()

    inputs = jnp.concatenate(
        [
            lax.dynamic_slice(residual, (source_layer, side * part, 0), (1, part, width))[0]
            for side in (width_index, 1 - width_index)
        ],
        axis=0,
    )
    partial_b = matmul(inputs, encoder[:, half:])
    leaving_b = partial_b[part:].astype(jnp.float16)
    arriving_b = across(leaving_b)
    leaving_a = matmul(inputs[part:], encoder[:, :half]).astype(jnp.float16)
    arriving_a = across(leaving_a)
    pre_b = add(partial_b[:part], arriving_b) + bias[half:]
    act_b = jnp.maximum(pre_b, 0.0).astype(jnp.bfloat16)
    sent = lax.ppermute(act_b, "feat", downward)
    sent_other = lax.ppermute(sent, ("feat", "width"), trailing_pairs)
    other_b = across(act_b)
    pre_a = add(matmul(inputs[:part], encoder[:, :half]), arriving_a) + bias[:half]
    act_a = jnp.maximum(pre_a, 0.0).astype(jnp.bfloat16)
    other_a = across(act_a)
    _, act_a, other_a = lax.optimization_barrier((sent, act_a, other_a))
    active = jnp.concatenate(
        [jnp.concatenate([act_a, act_b], axis=1), jnp.concatenate([other_a, other_b], axis=1)],
        axis=0,
    )
    active = lax.optimization_barrier(active)
    own_term = matmul(active, same_decoder)
    sent_other, own_term, sent = lax.optimization_barrier((sent_other, own_term, sent))
    order.start(
        0, summed_steps(own_term, first_plan, half_count, wanted_block(0, first_plan))
    )
    cross_input = jnp.where(leading, active[:, :half], jnp.concatenate([sent, sent_other], axis=0))
    cross_term = matmul(cross_input, next_decoder)
    second_part = jnp.where(leading, cross_term, own_term + cross_term)
    order.start(
        1, summed_steps(second_part, second_plan, feat_count, wanted_block(1, second_plan))
    )
    left = [len(plan) + len(plan) - 1 for plan in (first_plan, second_plan)]
    while left[1] > 0:
        for layer in (0, 1):
            if left[layer] > 0:
                order.advance(layer)
                left[layer] -= 1
    delta_first, delta_next = order.result(0), order.result(1)
    delta_own = jnp.where(leading, delta_first, delta_next)

    def back_parts(rows, delta_own, delta_next):
        cross = over_cols(delta_next[rows], next_decoder)
        back = over_cols(delta_own[rows], same_decoder[:half]) + jnp.where(leading, cross, 0.0)
        return cross, back, over_cols(delta_own[rows], same_decoder[half:])

    leaving = [
        block.astype(jnp.bfloat16) for block in back_parts(slice(part, None), delta_own, delta_next)
    ]
    cross_arriving = lax.ppermute(leaving[0], ("feat", "width"), trailing_pairs)
    arriving_a, arriving_b = across(leaving[1]), across(leaving[2])
    order.mark(*leaving)
    delta_own, delta_next = order.after((delta_own, delta_next))
    kept_cross, kept_a, kept_b = back_parts(slice(0, part), delta_own, delta_next)
    order.mark(kept_cross, kept_a, kept_b)
    kept_cross, cross_arriving = order.after((kept_cross, cross_arriving))
    cross_sum = add(kept_cross, cross_arriving).astype(jnp.bfloat16)
    returned = lax.ppermute(cross_sum, "feat", upward)
    order.mark(cross_sum)
    next_done = adamw_matmul(
        order.after(cross_input), delta_next, next_decoder, next_first, next_second, weight_decay
    )
    order.mark(*next_done)
    kept_a, arriving_a, pre_a = order.after((kept_a, arriving_a, pre_a))
    grad_a = jnp.where(pre_a > 0.0, add(kept_a, arriving_a), 0.0).astype(jnp.bfloat16)
    grad_other_a = across(grad_a)
    order.mark(grad_a)
    same_done = adamw_matmul(
        order.after(active), delta_own, same_decoder, same_first, same_second, weight_decay
    )
    order.mark(*same_done)
    kept_b, arriving_b, returned, pre_b = order.after((kept_b, arriving_b, returned, pre_b))
    total_b = add(add(kept_b, arriving_b), returned)
    grad_b = jnp.where(pre_b > 0.0, total_b, 0.0).astype(jnp.bfloat16)
    grad_other_b = across(grad_b)
    grad_sum = jnp.concatenate(
        [jnp.sum(grad.astype(jnp.float32), axis=0) for grad in (grad_a, grad_b)]
    )
    sum_other = across(grad_sum)
    order.mark(grad_b, grad_sum)
    grad_a, grad_other_a = order.after((grad_a, grad_other_a))
    encoder_done = adamw_matmul(
        inputs,
        jnp.concatenate([grad_a, grad_other_a], axis=0),
        encoder,
        encoder_first,
        encoder_second,
        weight_decay,
        (0, 2),
    )
    order.mark(*encoder_done)
    grad_b, grad_other_b, sum_other = order.after((grad_b, grad_other_b, sum_other))
    encoder_done = adamw_matmul(
        inputs,
        jnp.concatenate([grad_b, grad_other_b], axis=0),
        encoder,
        encoder_first,
        encoder_second,
        weight_decay,
        (1, 2),
        encoder_done,
    )
    grad_biases = grad_sum + sum_other
    updated_same, same_moment, same_square = same_done
    updated_next, next_moment, next_square = next_done
    updated_encoder, encoder_moment, encoder_square = encoder_done
    updated_biases, biases_moment, biases_square = adamw_update(
        biases, biases_first, biases_second, grad_biases, 0.0
    )
    return (
        updated_encoder,
        updated_biases,
        updated_same,
        updated_next,
        encoder_moment,
        encoder_square,
        biases_moment,
        biases_square,
        same_moment,
        same_square,
        next_moment,
        next_square,
    )


def solution(mesh):
    in_specs = (
        P(None, None, "width"),
        P(None, None, "width"),
        P("width", "feat"),
        P("feat"),
        P("feat", "width"),
        P("feat", "width"),
        P("width", "feat"),
        P("width", "feat"),
        P("feat"),
        P("feat"),
        P("feat", "width"),
        P("feat", "width"),
        P("feat", "width"),
        P("feat", "width"),
    )
    out_specs = (
        P("width", "feat"),
        P("feat"),
        P("feat", "width"),
        P("feat", "width"),
        P("width", "feat"),
        P("width", "feat"),
        P("feat"),
        P("feat"),
        P("feat", "width"),
        P("feat", "width"),
        P("feat", "width"),
        P("feat", "width"),
    )
    return jax.shard_map(local, mesh=mesh, in_specs=in_specs, out_specs=out_specs, check_vma=False)
```

```python
import functools
import math
import jax
import jax.numpy as jnp
from jax import lax
from jax.experimental import pallas as pl
from jax.experimental.pallas import tpu as pltpu
from jax.sharding import PartitionSpec as P

STEPS = 100


beta_one = 0.9
beta_two = 0.999
learn_rate = 0.002
adam_eps = 1e-08
weight_decay = 0.1


def adamw_update(parameter, first, second, gradient, decay_rate):
    first_new = beta_one * first.astype(jnp.float32) + (1.0 - beta_one) * gradient
    second_new = beta_two * second.astype(jnp.float32) + (1.0 - beta_two) * gradient * gradient
    first_hat = first_new / (1.0 - beta_one**STEPS)
    second_hat = second_new / (1.0 - beta_two**STEPS)
    weight = parameter.astype(jnp.float32)
    updated = weight - learn_rate * (
        first_hat / (jnp.sqrt(second_hat) + adam_eps) + decay_rate * weight
    )
    return (
        updated.astype(jnp.bfloat16),
        first_new.astype(jnp.bfloat16),
        second_new.astype(jnp.bfloat16),
    )


def adamw_kernel(decay_rate, tile, *refs):
    left_ref, right_ref, weight_ref, first_ref, second_ref = refs[:5]
    updated_ref, moment_ref, square_ref = refs[-3:]
    first_scale, second_scale = 1.0 - beta_one**STEPS, 1.0 - beta_two**STEPS
    keep = 1.0 - learn_rate * decay_rate
    rate = learn_rate * math.sqrt(second_scale) / first_scale
    shift = adam_eps * math.sqrt(second_scale)
    left = jnp.transpose(left_ref[...])
    for start in range(0, weight_ref.shape[1], tile):
        columns = slice(start, start + tile)
        gradient = matmul(left, right_ref[:, columns])
        scaled = (1.0 - beta_one) * gradient
        first_new = beta_one * first_ref[:, columns].astype(jnp.float32) + scaled
        second_new = (
            beta_two * second_ref[:, columns].astype(jnp.float32)
            + ((1.0 - beta_two) * gradient) * gradient
        )
        root = second_new * lax.rsqrt(second_new)
        step = (rate * first_new) * pl.reciprocal(root + shift, approx=True)
        updated = keep * weight_ref[:, columns].astype(jnp.float32) - step
        updated_ref[:, columns] = updated.astype(jnp.bfloat16)
        moment_ref[:, columns] = first_new.astype(jnp.bfloat16)
        square_ref[:, columns] = second_new.astype(jnp.bfloat16)


def adamw_matmul(left, right, weight, first, second, decay_rate, share=(0, 1), partly_done=()):
    tokens = left.shape[0]
    rows, width = weight.shape
    span = width // share[1]
    block = math.gcd(rows, 256 if span <= 1024 else 128)
    tile = math.gcd(span, 256)
    strip = pl.BlockSpec((block, span), lambda place: (place, share[0]))
    return pl.pallas_call(
        functools.partial(adamw_kernel, decay_rate, tile),
        grid=(rows // block,),
        in_specs=[
            pl.BlockSpec((tokens, block), lambda place: (0, place)),
            pl.BlockSpec((tokens, span), lambda place: (0, 0), pipeline_mode=pl.Buffered(1)),
            strip,
            strip,
            strip,
        ]
        + [pl.BlockSpec(memory_space=pl.ANY)] * len(partly_done),
        out_specs=[strip] * 3,
        out_shape=[jax.ShapeDtypeStruct((rows, width), jnp.bfloat16)] * 3,
        input_output_aliases={5 + at: at for at in range(len(partly_done))},
        compiler_params=pltpu.CompilerParams(vmem_limit_bytes=14 * 2**20),
        cost_estimate=pl.CostEstimate(
            flops=2 * tokens * rows * span,
            bytes_accessed=12 * rows * span,
            transcendentals=2 * rows * span,
        ),
    )(left, right, weight, first, second, *partly_done)


def matmul(left, right):
    return jnp.dot(left, right, preferred_element_type=jnp.float32)


def over_cols(left, right):
    return lax.dot_general(
        left, right, (((1,), (1,)), ((), ())), preferred_element_type=jnp.float32
    )


def across(value):
    return lax.ppermute(value, "width", [(0, 1), (1, 0)])


def flipped(value, bit, members):
    step = 1 << bit
    return lax.ppermute(value, "feat", [(index, index ^ step) for index in range(members)])


def halves(value, axis):
    size = value.shape[axis] // 2
    return lax.slice_in_dim(value, 0, size, axis=axis), lax.slice_in_dim(
        value, size, 2 * size, axis=axis
    )


def is_upper(bit):
    return ((lax.axis_index("feat") >> bit) & 1) == 1


def split_for(total, bit, axis):
    low, high = halves(total, axis)
    upper = is_upper(bit)
    return jnp.where(upper, high, low), jnp.where(upper, low, high).astype(jnp.bfloat16)


def joined(own, other, bit, axis):
    upper = is_upper(bit)
    return jnp.concatenate(
        [jnp.where(upper, other, own), jnp.where(upper, own, other)], axis=axis
    )


def plan_of(order):
    last = len(order) - 1
    return [
        (bit, None if place == last else 1 if place == 2 else 0)
        for place, bit in enumerate(order)
    ]


def add(total, arrived):
    return total + arrived.astype(jnp.float32)


def summed_steps(total, plan, members, wanted):
    for bit, axis in plan:
        if axis is None:
            keeping, leaving = total, total.astype(jnp.bfloat16)
        else:
            keeping, leaving = split_for(total, bit, axis)
        keeping, arrived = yield (leaving,), (keeping, flipped(leaving, bit, members))
        total = add(keeping, arrived)
    value = (total - wanted).astype(jnp.bfloat16)
    for bit, axis in reversed(plan):
        if axis is not None:
            value, other = yield (value,), (value, flipped(value, bit, members))
            value = joined(value, other, bit, axis)
    yield (value,), value


class Order:
    def __init__(self):
        self.last = ()
        self.waiting = {}

    def after(self, values):
        return lax.optimization_barrier((values, self.last))[0]

    def mark(self, *values):
        self.last = values

    def start(self, name, thread):
        self.last, pending = next(thread)
        self.waiting[name] = (thread, pending)

    def advance(self, name):
        thread, pending = self.waiting[name]
        self.last, pending = thread.send(self.after(pending))
        self.waiting[name] = (thread, pending)

    def result(self, name):
        return self.waiting[name][1]


def local(
    residual,
    targets,
    encoder,
    biases,
    same_decoder,
    next_decoder,
    encoder_first,
    encoder_second,
    biases_first,
    biases_second,
    same_first,
    same_second,
    next_first,
    next_second,
):
    feat_count = lax.axis_size("feat")
    feat_index = lax.axis_index("feat")
    width_index = lax.axis_index("width")
    half_count = feat_count // 2
    source_layer = feat_index // half_count
    leading = source_layer == 0
    tokens, width = residual.shape[1:]
    part = tokens // 2
    half = encoder.shape[1] // 2
    bias = biases.astype(jnp.float32)
    downward = [(index, index + half_count) for index in range(half_count)]
    upward = [(index + half_count, index) for index in range(half_count)]
    trailing_pairs = [
        (2 * index + side, 2 * index + 1 - side)
        for index in range(half_count, feat_count)
        for side in range(2)
    ]

    def wanted_block(layer, plan):
        starts, sizes = [0, 0], [tokens, width]
        for bit, axis in plan:
            if axis is not None:
                sizes[axis] //= 2
                starts[axis] = starts[axis] + is_upper(bit).astype(jnp.int32) * sizes[axis]
        row = lax.rem(starts[0] + width_index * part, tokens)
        block = lax.dynamic_slice(targets, (layer, row, starts[1]), (1, *sizes))
        return block[0].astype(jnp.float32)

    bits = feat_count.bit_length() - 1
    second_plan = plan_of(list(range(bits)))
    first_plan = plan_of([0, 2, 1] + list(range(3, bits - 1)))
    order = Order()

    inputs = jnp.concatenate(
        [
            lax.dynamic_slice(residual, (source_layer, side * part, 0), (1, part, width))[0]
            for side in (width_index, 1 - width_index)
        ],
        axis=0,
    )
    partial_b = matmul(inputs, encoder[:, half:])
    leaving_b = partial_b[part:].astype(jnp.float16)
    arriving_b = across(leaving_b)
    leaving_a = matmul(inputs[part:], encoder[:, :half]).astype(jnp.float16)
    arriving_a = across(leaving_a)
    pre_b = add(partial_b[:part], arriving_b) + bias[half:]
    act_b = jnp.maximum(pre_b, 0.0).astype(jnp.bfloat16)
    sent = lax.ppermute(act_b, "feat", downward)
    sent_other = lax.ppermute(sent, ("feat", "width"), trailing_pairs)
    other_b = across(act_b)
    pre_a = add(matmul(inputs[:part], encoder[:, :half]), arriving_a) + bias[:half]
    act_a = jnp.maximum(pre_a, 0.0).astype(jnp.bfloat16)
    other_a = across(act_a)
    _, act_a, other_a = lax.optimization_barrier((sent, act_a, other_a))
    active = jnp.concatenate(
        [jnp.concatenate([act_a, act_b], axis=1), jnp.concatenate([other_a, other_b], axis=1)],
        axis=0,
    )
    active = lax.optimization_barrier(active)
    own_term = matmul(active, same_decoder)
    sent_other, own_term, sent = lax.optimization_barrier((sent_other, own_term, sent))
    order.start(
        0, summed_steps(own_term, first_plan, half_count, wanted_block(0, first_plan))
    )
    cross_input = jnp.where(leading, active[:, :half], jnp.concatenate([sent, sent_other], axis=0))
    cross_term = matmul(cross_input, next_decoder)
    second_part = jnp.where(leading, cross_term, own_term + cross_term)
    order.start(
        1, summed_steps(second_part, second_plan, feat_count, wanted_block(1, second_plan))
    )
    left = [len(plan) + len(plan) - 1 for plan in (first_plan, second_plan)]
    while left[1] > 0:
        for layer in (1, 0):
            if left[layer] > 0:
                order.advance(layer)
                left[layer] -= 1
    delta_first, delta_next = order.result(0), order.result(1)
    delta_own = jnp.where(leading, delta_first, delta_next)

    def back_parts(rows, delta_own, delta_next):
        cross = over_cols(delta_next[rows], next_decoder)
        back = over_cols(delta_own[rows], same_decoder[:half]) + jnp.where(leading, cross, 0.0)
        return cross, back, over_cols(delta_own[rows], same_decoder[half:])

    leaving = [
        block.astype(jnp.bfloat16) for block in back_parts(slice(part, None), delta_own, delta_next)
    ]
    cross_arriving = lax.ppermute(leaving[0], ("feat", "width"), trailing_pairs)
    arriving_a, arriving_b = across(leaving[1]), across(leaving[2])
    order.mark(*leaving)
    delta_own, delta_next = order.after((delta_own, delta_next))
    kept_cross, kept_a, kept_b = back_parts(slice(0, part), delta_own, delta_next)
    order.mark(kept_cross, kept_a, kept_b)
    next_done = adamw_matmul(
        order.after(cross_input), delta_next, next_decoder, next_first, next_second, weight_decay
    )
    order.mark(*next_done)
    kept_cross, cross_arriving = order.after((kept_cross, cross_arriving))
    cross_sum = add(kept_cross, cross_arriving).astype(jnp.bfloat16)
    returned = lax.ppermute(cross_sum, "feat", upward)
    order.mark(cross_sum)
    kept_a, arriving_a, pre_a = order.after((kept_a, arriving_a, pre_a))
    grad_a = jnp.where(pre_a > 0.0, add(kept_a, arriving_a), 0.0).astype(jnp.bfloat16)
    grad_other_a = across(grad_a)
    order.mark(grad_a)
    same_done = adamw_matmul(
        order.after(active), delta_own, same_decoder, same_first, same_second, weight_decay
    )
    order.mark(*same_done)
    kept_b, arriving_b, returned, pre_b = order.after((kept_b, arriving_b, returned, pre_b))
    total_b = add(add(kept_b, arriving_b), returned)
    grad_b = jnp.where(pre_b > 0.0, total_b, 0.0).astype(jnp.bfloat16)
    grad_other_b = across(grad_b)
    grad_sum = jnp.concatenate(
        [jnp.sum(grad.astype(jnp.float32), axis=0) for grad in (grad_a, grad_b)]
    )
    sum_other = across(grad_sum)
    order.mark(grad_b, grad_sum)
    grad_a, grad_other_a = order.after((grad_a, grad_other_a))
    encoder_done = adamw_matmul(
        inputs,
        jnp.concatenate([grad_a, grad_other_a], axis=0),
        encoder,
        encoder_first,
        encoder_second,
        weight_decay,
        (0, 2),
    )
    order.mark(*encoder_done)
    grad_b, grad_other_b, sum_other = order.after((grad_b, grad_other_b, sum_other))
    encoder_done = adamw_matmul(
        inputs,
        jnp.concatenate([grad_b, grad_other_b], axis=0),
        encoder,
        encoder_first,
        encoder_second,
        weight_decay,
        (1, 2),
        encoder_done,
    )
    grad_biases = grad_sum + sum_other
    updated_same, same_moment, same_square = same_done
    updated_next, next_moment, next_square = next_done
    updated_encoder, encoder_moment, encoder_square = encoder_done
    updated_biases, biases_moment, biases_square = adamw_update(
        biases, biases_first, biases_second, grad_biases, 0.0
    )
    return (
        updated_encoder,
        updated_biases,
        updated_same,
        updated_next,
        encoder_moment,
        encoder_square,
        biases_moment,
        biases_square,
        same_moment,
        same_square,
        next_moment,
        next_square,
    )


def solution(mesh):
    in_specs = (
        P(None, None, "width"),
        P(None, None, "width"),
        P("width", "feat"),
        P("feat"),
        P("feat", "width"),
        P("feat", "width"),
        P("width", "feat"),
        P("width", "feat"),
        P("feat"),
        P("feat"),
        P("feat", "width"),
        P("feat", "width"),
        P("feat", "width"),
        P("feat", "width"),
    )
    out_specs = (
        P("width", "feat"),
        P("feat"),
        P("feat", "width"),
        P("feat", "width"),
        P("width", "feat"),
        P("width", "feat"),
        P("feat"),
        P("feat"),
        P("feat", "width"),
        P("feat", "width"),
        P("feat", "width"),
        P("feat", "width"),
    )
    return jax.shard_map(local, mesh=mesh, in_specs=in_specs, out_specs=out_specs, check_vma=False)
```

```python
import functools
import math
import jax
import jax.numpy as jnp
from jax import lax
from jax.experimental import pallas as pl
from jax.experimental.pallas import tpu as pltpu
from jax.sharding import PartitionSpec as P

STEPS = 100


beta_one = 0.9
beta_two = 0.999
learn_rate = 0.002
adam_eps = 1e-08
weight_decay = 0.1


def adamw_update(parameter, first, second, gradient, decay_rate):
    first_new = beta_one * first.astype(jnp.float32) + (1.0 - beta_one) * gradient
    second_new = beta_two * second.astype(jnp.float32) + (1.0 - beta_two) * gradient * gradient
    first_hat = first_new / (1.0 - beta_one**STEPS)
    second_hat = second_new / (1.0 - beta_two**STEPS)
    weight = parameter.astype(jnp.float32)
    updated = weight - learn_rate * (
        first_hat / (jnp.sqrt(second_hat) + adam_eps) + decay_rate * weight
    )
    return (
        updated.astype(jnp.bfloat16),
        first_new.astype(jnp.bfloat16),
        second_new.astype(jnp.bfloat16),
    )


def adamw_kernel(decay_rate, tile, *refs):
    left_ref, right_ref, weight_ref, first_ref, second_ref = refs[:5]
    updated_ref, moment_ref, square_ref = refs[-3:]
    first_scale, second_scale = 1.0 - beta_one**STEPS, 1.0 - beta_two**STEPS
    keep = 1.0 - learn_rate * decay_rate
    rate = learn_rate * math.sqrt(second_scale) / first_scale
    shift = adam_eps * math.sqrt(second_scale)
    left = jnp.transpose(left_ref[...])
    for start in range(0, weight_ref.shape[1], tile):
        columns = slice(start, start + tile)
        gradient = matmul(left, right_ref[:, columns])
        scaled = (1.0 - beta_one) * gradient
        first_new = beta_one * first_ref[:, columns].astype(jnp.float32) + scaled
        second_new = (
            beta_two * second_ref[:, columns].astype(jnp.float32)
            + ((1.0 - beta_two) * gradient) * gradient
        )
        root = second_new * lax.rsqrt(second_new)
        step = (rate * first_new) * pl.reciprocal(root + shift, approx=True)
        updated = keep * weight_ref[:, columns].astype(jnp.float32) - step
        updated_ref[:, columns] = updated.astype(jnp.bfloat16)
        moment_ref[:, columns] = first_new.astype(jnp.bfloat16)
        square_ref[:, columns] = second_new.astype(jnp.bfloat16)


def adamw_matmul(left, right, weight, first, second, decay_rate, share=(0, 1), partly_done=()):
    tokens = left.shape[0]
    rows, width = weight.shape
    span = width // share[1]
    block = math.gcd(rows, 256)
    tile = math.gcd(span, 256)
    strip = pl.BlockSpec((block, span), lambda place: (place, share[0]))
    return pl.pallas_call(
        functools.partial(adamw_kernel, decay_rate, tile),
        grid=(rows // block,),
        in_specs=[
            pl.BlockSpec((tokens, block), lambda place: (0, place)),
            pl.BlockSpec((tokens, span), lambda place: (0, 0), pipeline_mode=pl.Buffered(1)),
            strip,
            strip,
            strip,
        ]
        + [pl.BlockSpec(memory_space=pl.ANY)] * len(partly_done),
        out_specs=[strip] * 3,
        out_shape=[jax.ShapeDtypeStruct((rows, width), jnp.bfloat16)] * 3,
        input_output_aliases={5 + at: at for at in range(len(partly_done))},
        compiler_params=pltpu.CompilerParams(vmem_limit_bytes=18 * 2**20),
        cost_estimate=pl.CostEstimate(
            flops=2 * tokens * rows * span,
            bytes_accessed=12 * rows * span,
            transcendentals=2 * rows * span,
        ),
    )(left, right, weight, first, second, *partly_done)


def matmul(left, right):
    return jnp.dot(left, right, preferred_element_type=jnp.float32)


def over_cols(left, right):
    return lax.dot_general(
        left, right, (((1,), (1,)), ((), ())), preferred_element_type=jnp.float32
    )


def across(value):
    return lax.ppermute(value, "width", [(0, 1), (1, 0)])


def flipped(value, bit, members):
    step = 1 << bit
    return lax.ppermute(value, "feat", [(index, index ^ step) for index in range(members)])


def halves(value, axis):
    size = value.shape[axis] // 2
    return lax.slice_in_dim(value, 0, size, axis=axis), lax.slice_in_dim(
        value, size, 2 * size, axis=axis
    )


def is_upper(bit):
    return ((lax.axis_index("feat") >> bit) & 1) == 1


def split_for(total, bit, axis):
    low, high = halves(total, axis)
    upper = is_upper(bit)
    return jnp.where(upper, high, low), jnp.where(upper, low, high).astype(jnp.bfloat16)


def joined(own, other, bit, axis):
    upper = is_upper(bit)
    return jnp.concatenate(
        [jnp.where(upper, other, own), jnp.where(upper, own, other)], axis=axis
    )


def plan_of(order):
    last = len(order) - 1
    return [
        (bit, None if place == last else 1 if place == 2 else 0)
        for place, bit in enumerate(order)
    ]


def add(total, arrived):
    return total + arrived.astype(jnp.float32)


def summed_steps(total, plan, members, wanted):
    for bit, axis in plan:
        if axis is None:
            keeping, leaving = total, total.astype(jnp.bfloat16)
        else:
            keeping, leaving = split_for(total, bit, axis)
        keeping, arrived = yield (leaving,), (keeping, flipped(leaving, bit, members))
        total = add(keeping, arrived)
    value = (total - wanted).astype(jnp.bfloat16)
    for bit, axis in reversed(plan):
        if axis is not None:
            value, other = yield (value,), (value, flipped(value, bit, members))
            value = joined(value, other, bit, axis)
    yield (value,), value


class Order:
    def __init__(self):
        self.last = ()
        self.waiting = {}

    def after(self, values):
        return lax.optimization_barrier((values, self.last))[0]

    def mark(self, *values):
        self.last = values

    def start(self, name, thread):
        self.last, pending = next(thread)
        self.waiting[name] = (thread, pending)

    def advance(self, name):
        thread, pending = self.waiting[name]
        self.last, pending = thread.send(self.after(pending))
        self.waiting[name] = (thread, pending)

    def result(self, name):
        return self.waiting[name][1]


def local(
    residual,
    targets,
    encoder,
    biases,
    same_decoder,
    next_decoder,
    encoder_first,
    encoder_second,
    biases_first,
    biases_second,
    same_first,
    same_second,
    next_first,
    next_second,
):
    feat_count = lax.axis_size("feat")
    feat_index = lax.axis_index("feat")
    width_index = lax.axis_index("width")
    half_count = feat_count // 2
    source_layer = feat_index // half_count
    leading = source_layer == 0
    tokens, width = residual.shape[1:]
    part = tokens // 2
    half = encoder.shape[1] // 2
    bias = biases.astype(jnp.float32)
    downward = [(index, index + half_count) for index in range(half_count)]
    upward = [(index + half_count, index) for index in range(half_count)]
    trailing_pairs = [
        (2 * index + side, 2 * index + 1 - side)
        for index in range(half_count, feat_count)
        for side in range(2)
    ]

    def wanted_block(layer, plan):
        starts, sizes = [0, 0], [tokens, width]
        for bit, axis in plan:
            if axis is not None:
                sizes[axis] //= 2
                starts[axis] = starts[axis] + is_upper(bit).astype(jnp.int32) * sizes[axis]
        row = lax.rem(starts[0] + width_index * part, tokens)
        block = lax.dynamic_slice(targets, (layer, row, starts[1]), (1, *sizes))
        return block[0].astype(jnp.float32)

    bits = feat_count.bit_length() - 1
    second_plan = plan_of(list(range(bits)))
    first_plan = plan_of([0, 2, 1] + list(range(3, bits - 1)))
    order = Order()

    inputs = jnp.concatenate(
        [
            lax.dynamic_slice(residual, (source_layer, side * part, 0), (1, part, width))[0]
            for side in (width_index, 1 - width_index)
        ],
        axis=0,
    )
    partial_b = matmul(inputs, encoder[:, half:])
    leaving_b = partial_b[part:].astype(jnp.float16)
    arriving_b = across(leaving_b)
    leaving_a = matmul(inputs[part:], encoder[:, :half]).astype(jnp.float16)
    arriving_a = across(leaving_a)
    pre_b = add(partial_b[:part], arriving_b) + bias[half:]
    act_b = jnp.maximum(pre_b, 0.0).astype(jnp.bfloat16)
    sent = lax.ppermute(act_b, "feat", downward)
    sent_other = lax.ppermute(sent, ("feat", "width"), trailing_pairs)
    other_b = across(act_b)
    pre_a = add(matmul(inputs[:part], encoder[:, :half]), arriving_a) + bias[:half]
    act_a = jnp.maximum(pre_a, 0.0).astype(jnp.bfloat16)
    other_a = across(act_a)
    _, act_a, other_a = lax.optimization_barrier((sent, act_a, other_a))
    active = jnp.concatenate(
        [jnp.concatenate([act_a, act_b], axis=1), jnp.concatenate([other_a, other_b], axis=1)],
        axis=0,
    )
    active = lax.optimization_barrier(active)
    own_term = matmul(active, same_decoder)
    sent_other, own_term, sent = lax.optimization_barrier((sent_other, own_term, sent))
    order.start(
        0, summed_steps(own_term, first_plan, half_count, wanted_block(0, first_plan))
    )
    cross_input = jnp.where(leading, active[:, :half], jnp.concatenate([sent, sent_other], axis=0))
    cross_term = matmul(cross_input, next_decoder)
    second_part = jnp.where(leading, cross_term, own_term + cross_term)
    order.start(
        1, summed_steps(second_part, second_plan, feat_count, wanted_block(1, second_plan))
    )
    turns = [1, 0] * len(first_plan) + [1] + [1, 0] * (len(first_plan) - 1) + [1]
    for layer in turns:
        order.advance(layer)
    delta_first, delta_next = order.result(0), order.result(1)
    delta_own = jnp.where(leading, delta_first, delta_next)

    def back_parts(rows, delta_own, delta_next):
        cross = over_cols(delta_next[rows], next_decoder)
        back = over_cols(delta_own[rows], same_decoder[:half]) + jnp.where(leading, cross, 0.0)
        return cross, back, over_cols(delta_own[rows], same_decoder[half:])

    leaving = [
        block.astype(jnp.bfloat16) for block in back_parts(slice(part, None), delta_own, delta_next)
    ]
    cross_arriving = lax.ppermute(leaving[0], ("feat", "width"), trailing_pairs)
    arriving_a, arriving_b = across(leaving[1]), across(leaving[2])
    order.mark(*leaving)
    delta_own, delta_next = order.after((delta_own, delta_next))
    kept_cross, kept_a, kept_b = back_parts(slice(0, part), delta_own, delta_next)
    order.mark(kept_cross, kept_a, kept_b)
    next_done = adamw_matmul(
        order.after(cross_input), delta_next, next_decoder, next_first, next_second, weight_decay
    )
    order.mark(*next_done)
    kept_cross, cross_arriving = order.after((kept_cross, cross_arriving))
    cross_sum = add(kept_cross, cross_arriving).astype(jnp.bfloat16)
    returned = lax.ppermute(cross_sum, "feat", upward)
    order.mark(cross_sum)
    kept_a, arriving_a, pre_a = order.after((kept_a, arriving_a, pre_a))
    grad_a = jnp.where(pre_a > 0.0, add(kept_a, arriving_a), 0.0).astype(jnp.bfloat16)
    grad_other_a = across(grad_a)
    order.mark(grad_a)
    same_done = adamw_matmul(
        order.after(active), delta_own, same_decoder, same_first, same_second, weight_decay
    )
    order.mark(*same_done)
    kept_b, arriving_b, returned, pre_b = order.after((kept_b, arriving_b, returned, pre_b))
    total_b = add(add(kept_b, arriving_b), returned)
    grad_b = jnp.where(pre_b > 0.0, total_b, 0.0).astype(jnp.bfloat16)
    grad_other_b = across(grad_b)
    grad_sum = jnp.concatenate(
        [jnp.sum(grad.astype(jnp.float32), axis=0) for grad in (grad_a, grad_b)]
    )
    sum_other = across(grad_sum)
    order.mark(grad_b, grad_sum)
    grad_a, grad_other_a = order.after((grad_a, grad_other_a))
    encoder_done = adamw_matmul(
        inputs,
        jnp.concatenate([grad_a, grad_other_a], axis=0),
        encoder,
        encoder_first,
        encoder_second,
        weight_decay,
        (0, 2),
    )
    order.mark(*encoder_done)
    grad_b, grad_other_b, sum_other = order.after((grad_b, grad_other_b, sum_other))
    encoder_done = adamw_matmul(
        inputs,
        jnp.concatenate([grad_b, grad_other_b], axis=0),
        encoder,
        encoder_first,
        encoder_second,
        weight_decay,
        (1, 2),
        encoder_done,
    )
    grad_biases = grad_sum + sum_other
    updated_same, same_moment, same_square = same_done
    updated_next, next_moment, next_square = next_done
    updated_encoder, encoder_moment, encoder_square = encoder_done
    updated_biases, biases_moment, biases_square = adamw_update(
        biases, biases_first, biases_second, grad_biases, 0.0
    )
    return (
        updated_encoder,
        updated_biases,
        updated_same,
        updated_next,
        encoder_moment,
        encoder_square,
        biases_moment,
        biases_square,
        same_moment,
        same_square,
        next_moment,
        next_square,
    )


def solution(mesh):
    in_specs = (
        P(None, None, "width"),
        P(None, None, "width"),
        P("width", "feat"),
        P("feat"),
        P("feat", "width"),
        P("feat", "width"),
        P("width", "feat"),
        P("width", "feat"),
        P("feat"),
        P("feat"),
        P("feat", "width"),
        P("feat", "width"),
        P("feat", "width"),
        P("feat", "width"),
    )
    out_specs = (
        P("width", "feat"),
        P("feat"),
        P("feat", "width"),
        P("feat", "width"),
        P("width", "feat"),
        P("width", "feat"),
        P("feat"),
        P("feat"),
        P("feat", "width"),
        P("feat", "width"),
        P("feat", "width"),
        P("feat", "width"),
    )
    return jax.shard_map(local, mesh=mesh, in_specs=in_specs, out_specs=out_specs, check_vma=False)
```
